256 devices in a mesh: sfc: 64 (over z, y, core), lev: 4 (over x).
Axes of the slice: x: 4, y: 4, z: 8, core: 2. Of those that a mesh axis runs over, the one named last changes fastest.
Arguments:
- tracers: float32 [16, 40, 32768], P('lev', None, 'sfc'), may hold values from 0.1 to 4
- owners: int32 [2, 16, 32768], P(None, 'lev', 'sfc'), may hold values from 0 to 63, as said below
- source_elements: int32 [2, 16, 32768], P(None, 'lev', 'sfc'), may hold values from 0 to 31, as said below
- ref_coords: float32 [2, 2, 16, 32768], P(None, None, 'lev', 'sfc'), may hold values from -1 to 1
- node_mass: float32 [32768], P('sfc'), may hold values from 0.4 to 2.5
- neighbours: int32 [3, 32768], P(None, 'sfc'), may hold values from -1 to 32767, as said below
- lift_fraction: float32 [16, 32768], P('lev', 'sfc'), may hold values from 0 to 0.8
Outputs:
- transported: float32 [16, 40, 32768], P('lev', None, 'sfc')
The draws below stay inside these ranges and needn't reach their ends.
Inputs may be any that keep to these rules, and one draw needn't show every extreme that they name: Elements form a torus of 256 rows by 8 columns numbered row by row; block b holds rows 4 b to 4 b + 3. The source element named by owners and source_elements is the node's own element or one of its eight neighbours on this torus, so the owner is the node's block, the previous or the next one (the last block's next is the first). In every substep and level, at most 128 nodes of one block name the previous block and at most 128 the next; each bound is reached by some block. `source_elements`: drawn together with owners, as described there. Each entry is -1 or the index of another copy of the same grid point; copies name each other; a node has 0, 1 or 3 other copies. The element of a copy is one of the eight neighbours of the node's element on the torus described for owners.
All inputs are finite; a program needn't handle non-finite values.
Results may differ from the reference program's by a relative error of at most 0.0001.
Values sent between devices are 32-bit elements; how exact they have to be, the bound alone decides.
A program may use at most 128 MiB of HBM per device.

```python
import math
import jax
import jax.numpy as jnp
from jax import lax

STRIP = 8
NODES = 16
TRACERS = 40
SUB = 2
EL = 32
ELEMENTS = 2048
LEVELS = 16
NPTS = 32768
N_SFC = 64


def departure(key):
    row_total = ELEMENTS // STRIP
    base = jax.random.fold_in(key, 7)
    key_row, key_col, key_down, key_up = jax.random.split(base, 4)
    shape = (SUB, LEVELS, ELEMENTS, NODES)
    steps_table = jnp.array([-1, -1, 0, 1, 1], dtype=jnp.int32)
    row_step = steps_table[jax.random.randint(key_row, shape, 0, 5)]
    col_step = jax.random.randint(key_col, shape, -1, 2)
    elem_ids = jnp.arange(ELEMENTS, dtype=jnp.int32)
    grid_row = elem_ids // STRIP
    grid_col = elem_ids % STRIP
    block_of = (grid_row // 4)[None, None, :, None]
    inner_row = (grid_row % 4)[None, None, :, None]
    pick_down = jax.random.randint(key_down, (SUB, LEVELS, 1, 1), 0, N_SFC)
    pick_up = jax.random.randint(key_up, (SUB, LEVELS, 1, 1), 0, N_SFC)
    row_step = jnp.where((block_of == pick_down) & (inner_row == 0), -1, row_step)
    row_step = jnp.where((block_of == pick_up) & (inner_row == 3), 1, row_step)
    new_row = jnp.mod(grid_row[None, None, :, None] + row_step, row_total)
    new_col = jnp.mod(grid_col[None, None, :, None] + col_step, STRIP)
    owner = new_row // 4
    inside = new_row % 4 * STRIP + new_col
    return (owner.reshape(SUB, LEVELS, NPTS).astype(jnp.int32), inside.reshape(SUB, LEVELS, NPTS).astype(jnp.int32))


def draw_owners(key, part):
    return departure(key)[0]


def draw_source_elements(key, part):
    return departure(key)[1]


def draw_neighbours(key, part):
    row_total = ELEMENTS // STRIP
    rotation = jax.random.randint(key, (ELEMENTS,), 0, 4)
    elem_ids = jnp.arange(ELEMENTS, dtype=jnp.int32)
    grid_row = elem_ids // STRIP
    grid_col = elem_ids % STRIP
    node_ids = jnp.arange(16, dtype=jnp.int32)
    along_i = node_ids // 4
    along_j = node_ids % 4
    first_opts = jnp.stack([along_i, along_j, 3 - along_i, 3 - along_j])
    second_opts = jnp.stack([along_j, 3 - along_i, 3 - along_j, along_i])
    canon_u = first_opts[rotation]
    canon_v = second_opts[rotation]
    lattice_x = (3 * grid_row[:, None] + canon_u) % (3 * row_total)
    lattice_y = (3 * grid_col[:, None] + canon_v) % (3 * STRIP)
    point_key = lattice_x * (3 * STRIP) + lattice_y
    shifts = [(-1, -1), (-1, 0), (-1, 1), (0, -1), (0, 1), (1, -1), (1, 0), (1, 1)]
    nearby = jnp.stack([(grid_row + shift_r) % row_total * STRIP + (grid_col + shift_c) % STRIP for shift_r, shift_c in shifts], axis=1)
    cand_key = point_key[nearby].reshape(ELEMENTS, 128)
    cand_id = (nearby[:, :, None] * 16 + node_ids[None, None, :]).reshape(ELEMENTS, 128)
    matches = point_key[:, :, None] == cand_key[:, None, :]
    running = jnp.cumsum(matches.astype(jnp.int32), axis=-1)
    copies = []
    for copy_no in range(3):
        picked = matches & (running == copy_no + 1)
        found = jnp.any(picked, axis=-1)
        value = jnp.sum(jnp.where(picked, cand_id[:, None, :], 0), axis=-1)
        copies.append(jnp.where(found, value, -1))
    return jnp.stack(copies).reshape(3, ELEMENTS * 16).astype(jnp.int32)


def shard_levels(rng, extent, pieces, low, high):
    level = 1.0
    for dim, parts in pieces:
        heights = jax.random.uniform(jax.random.fold_in(jax.random.fold_in(rng, 6), dim), (parts,), jnp.float32, low / len(pieces), high / len(pieces))
        level = level * jnp.repeat(jnp.exp(heights), extent[dim] // parts).reshape((-1,) + (1,) * (len(extent) - 1 - dim))
    return level


def setup_inputs(seed: int = 0) -> dict:
    key_list = jax.random.split(jax.random.key(seed), 8)
    tracers = jnp.clip(jnp.exp(math.log(4.0) - 3.6888794 * jax.random.uniform(key_list[0], (LEVELS, TRACERS, NPTS), jnp.float32) ** shard_levels(key_list[0], (LEVELS, TRACERS, NPTS), ((0, 4), (2, 64)), -0.2, 0.2)), 0.1, 4.0)
    owners = draw_owners(jax.random.fold_in(key_list[7], 71), 0)
    source_elements = draw_source_elements(jax.random.fold_in(key_list[7], 71), 0)
    ref_coords = jnp.clip(jax.random.uniform(key_list[3], (SUB, 2, LEVELS, NPTS), jnp.float32, -1.0, 1.0) * shard_levels(key_list[3], (SUB, 2, LEVELS, NPTS), ((2, 4), (3, 64)), -0.4, 0.0), -1.0, 1.0)
    node_mass = jnp.clip(jnp.exp(math.log(2.5) - 1.8325814 * jax.random.uniform(key_list[4], (NPTS,), jnp.float32) ** shard_levels(key_list[4], (NPTS,), ((0, 64),), -0.2, 0.2)), 0.4, 2.5)
    neighbours = draw_neighbours(jax.random.fold_in(key_list[7], 71), 0)
    lift_fraction = jnp.clip(0.8 * jax.random.uniform(key_list[6], (LEVELS, NPTS), jnp.float32) ** shard_levels(key_list[6], (LEVELS, NPTS), ((0, 4), (1, 64)), -0.2, 0.2), 0.0, 0.8)
    return {"tracers": tracers, "owners": owners, "source_elements": source_elements, "ref_coords": ref_coords, "node_mass": node_mass, "neighbours": neighbours, "lift_fraction": lift_fraction}


GLL_POINTS = (-1.0, -0.4472135954999579, 0.4472135954999579, 1.0)


def basis(position):
    columns = []
    for node_i in range(4):
        factor = jnp.ones_like(position)
        for node_k in range(4):
            if node_k != node_i:
                factor = factor * ((position - GLL_POINTS[node_k]) / (GLL_POINTS[node_i] - GLL_POINTS[node_k]))
        columns.append(factor)
    return jnp.stack(columns, axis=0)


def node_weights(coord_a, coord_b):
    outer = basis(coord_a)[:, None] * basis(coord_b)[None, :]
    return outer.reshape((16,) + coord_a.shape)


def interp_level(packed):
    level_field, elem_index, weights = packed
    tracer_count = level_field.shape[0]
    grouped = level_field.reshape(tracer_count, -1, 16)[:, elem_index, :]
    return jnp.einsum("np,qpn->qp", weights, grouped, precision=lax.Precision.HIGHEST)


def smooth_edges(moved, node_mass, neighbours):
    weighted = moved * node_mass[None, None, :]
    total = weighted
    mass_sum = node_mass
    for copy_no in range(3):
        target = neighbours[copy_no]
        usable = target >= 0
        safe_target = jnp.where(usable, target, 0)
        total = total + jnp.where(usable[None, None, :], weighted[:, :, safe_target], 0.0)
        mass_sum = mass_sum + jnp.where(usable, node_mass[safe_target], 0.0)
    return total / mass_sum[None, None, :]


def reference(tracers, owners, source_elements, ref_coords, node_mass, neighbours, lift_fraction):
    tracer_field = tracers
    for step_no in range(SUB):
        source_global = owners[step_no] * EL + source_elements[step_no]
        weights = node_weights(ref_coords[step_no, 0], ref_coords[step_no, 1])
        weights = jnp.moveaxis(weights, 0, 1)
        moved = lax.map(interp_level, (tracer_field, source_global, weights))
        tracer_field = smooth_edges(moved, node_mass, neighbours)
    upper = jnp.concatenate([tracer_field[1:], tracer_field[-1:]], axis=0)
    fraction = lift_fraction[:, None, :]
    return tracer_field + fraction * (upper - tracer_field)
```

```python
import functools

import jax
import jax.numpy as jnp
from jax import lax
from jax.experimental import pallas as pl
from jax.experimental.pallas import tpu as pltpu
from jax.sharding import PartitionSpec as P

GLL_POINTS = (-1.0, -0.4472135954999579, 0.4472135954999579, 1.0)
MESH = pl.DeviceIdType.MESH
BF16 = jnp.bfloat16
F32 = jnp.float32
LEVELS = 4
TRACERS = 40
ROW = 128
BLOCK = 512


def basis_tables():
    node = lax.broadcasted_iota(jnp.int32, (16, ROW), 0)

    def pick(index, values):
        out = jnp.full((16, ROW), values[3], F32)
        for k in range(3):
            out = jnp.where(index == k, values[k], out)
        return out

    others = [[x for k, x in enumerate(GLL_POINTS) if k != i] for i in range(4)]
    scale = []
    for i in range(4):
        product = 1.0
        for x in others[i]:
            product *= GLL_POINTS[i] - x
        scale.append(1.0 / product)
    first, second = node >> 2, node & 3
    points_a = [pick(first, [others[i][k] for i in range(4)]) for k in range(3)]
    points_b = [pick(second, [others[i][k] for i in range(4)]) for k in range(3)]
    return points_a, points_b, pick(first, scale) * pick(second, scale)


def split(values):
    high = values.astype(BF16).astype(F32)
    return jnp.concatenate([high, values - high], axis=0).astype(BF16)


def spread(row):
    return jnp.broadcast_to(row, (16, ROW))


def kernel(
    tracers, owners, elements, coords, mass, neighbours, lift,
    out,
    field_prev, field_own, field_next, own_ids, elem_ids, refs, masses, copies, lifts, prepared,
    weights1, weights2, shared, inverse, stage0, stage1, stage2, stage3, result, above,
    local_sem, send_dep, recv_dep, send_field, recv_field, send_up, recv_up,
):
    me = lax.axis_index("sfc")
    peers = lax.axis_size("sfc")
    group = lax.axis_index("lev")
    groups = lax.axis_size("lev")
    after = lax.rem(me + 1, peers)
    before = lax.rem(me + peers - 1, peers)

    barrier = pltpu.get_barrier_semaphore()
    for device in (before, after):
        pl.semaphore_signal(barrier, inc=1, device_id={"sfc": device}, device_id_type=MESH)

    @pl.when(group < groups - 1)
    def _():
        pl.semaphore_signal(barrier, inc=1, device_id={"lev": group + 1}, device_id_type=MESH)

    local = []

    def fetch(source, target):
        copy = pltpu.make_async_copy(source, target, local_sem.at[len(local)])
        copy.start()
        local.append(copy)

    fetch(owners, own_ids.at[1])
    fetch(elements, elem_ids.at[1])
    fetch(coords, refs.at[1])
    fetch(mass, masses.at[1])
    fetch(neighbours, copies.at[1])
    fetch(lift, lifts)
    fetch(tracers, field_own)

    pl.semaphore_wait(barrier, jnp.where(group > 0, 3, 2))

    sides = ((after, 0, BLOCK - ROW, field_prev), (before, 2, 0, field_next))
    deps = []
    for side, (device, slot, edge, _) in enumerate(sides):
        pieces = (
            (owners.at[0], own_ids.at[slot, 0]),
            (elements.at[0], elem_ids.at[slot, 0]),
            (coords.at[0], refs.at[slot, 0]),
            (mass, masses.at[slot]),
            (neighbours, copies.at[slot]),
            (owners.at[1, :, pl.ds(edge, ROW)], own_ids.at[slot, 1, :, pl.ds(edge, ROW)]),
            (elements.at[1, :, pl.ds(edge, ROW)], elem_ids.at[slot, 1, :, pl.ds(edge, ROW)]),
            (coords.at[1, :, :, pl.ds(edge, ROW)], refs.at[slot, 1, :, :, pl.ds(edge, ROW)]),
        )
        deps.append(
            [
                pltpu.make_async_remote_copy(
                    src_ref=source,
                    dst_ref=target,
                    send_sem=send_dep.at[side, number],
                    recv_sem=recv_dep.at[side, number],
                    device_id={"sfc": device},
                    device_id_type=MESH,
                )
                for number, (source, target) in enumerate(pieces)
            ]
        )
    for pair in zip(*deps):
        for copy in pair:
            copy.start()

    def field_copy(side, level):
        device, _, _, target = sides[side]
        return pltpu.make_async_remote_copy(
            src_ref=tracers.at[level],
            dst_ref=target.at[level],
            send_sem=send_field.at[side, level],
            recv_sem=recv_field.at[side, level],
            device_id={"sfc": device},
            device_id_type=MESH,
        )

    for level in range(LEVELS):
        for side in range(2):
            field_copy(side, level).start()

    points_a, points_b, scale = basis_tables()
    row_mask = 4 * peers - 1
    point_mask = BLOCK * peers - 1
    node = lax.broadcasted_iota(jnp.int32, (16, ROW), 0)
    lane = lax.broadcasted_iota(jnp.int32, (16, ROW), 1)
    zero = jnp.zeros((16, ROW), BF16)
    own_elem = (8 + (lane >> 4)).astype(F32).astype(BF16)
    own_pick = jnp.where((lane & 15) == node, 1.0, 0.0).astype(BF16)

    def prepare(slot, step, rows):
        lanes = pl.ds(rows[0] * ROW, len(rows) * ROW)
        width = len(rows) * ROW
        row = lax.broadcasted_iota(jnp.int32, (LEVELS, width), 1) // ROW + rows[0]
        elem = elem_ids[slot, step, :, lanes]
        source_row = own_ids[slot, step, :, lanes] * 4 + (elem >> 3)
        above_row = (me + (slot - 1)) * 4 - 1 + row
        offset = (source_row - above_row) & row_mask
        code = (offset * 8 + (elem & 7)).astype(F32)
        for level in range(LEVELS):
            prepared[slot, step, level, 0:1, lanes] = code[level : level + 1]
            prepared[slot, step, level, 1:2, lanes] = refs[slot, step, 0, level : level + 1, lanes]
            prepared[slot, step, level, 2:3, lanes] = refs[slot, step, 1, level : level + 1, lanes]

    def build_weights(slot, row, step, level, target, pair, place):
        lanes = pl.ds(row * ROW, ROW)
        code = spread(prepared[slot, step, level, 0:1, lanes]).astype(BF16)
        a = spread(prepared[slot, step, level, 1:2, lanes])
        b = spread(prepared[slot, step, level, 2:3, lanes])
        weight = spread(masses[slot, :, lanes]) * scale
        for point in points_a:
            weight = weight * (a - point)
        for point in points_b:
            weight = weight * (b - point)
        high = weight.astype(BF16)
        low = (weight - high.astype(F32)).astype(BF16)
        start = ROW * place
        for number in range(24):
            hit = code == jnp.asarray(number, BF16)
            rows = pl.ds(start + 16 * number, 16)
            target[level, pair, rows, pl.ds(start, ROW)] = jnp.where(hit, high, zero)
            target[level, pair, rows, pl.ds(256 + start, ROW)] = jnp.where(hit, low, zero)
        blank = jnp.zeros((ROW, ROW), BF16)
        rows = pl.ds(0 if place else 384, ROW)
        target[level, pair, rows, pl.ds(start, ROW)] = blank
        target[level, pair, rows, pl.ds(256 + start, ROW)] = blank

    def build_shared(slot, row, pair, place):
        lanes = pl.ds(row * ROW, ROW)
        first = ((me + (slot - 1)) * 4 + (row - 1)) * ROW
        codes, picks = [], []
        for number in range(3):
            copy = copies[slot, pl.ds(number, 1), lanes]
            offset = (copy - first) & point_mask
            code = jnp.where(copy >= 0, offset >> 4, -1)
            codes.append(spread(code.astype(F32)).astype(BF16))
            picks.append(jnp.where(spread(offset & 15) == node, 1.0, 0.0).astype(BF16))
        start = ROW * place
        for number in range(24):
            count = jnp.asarray(number, BF16)
            value = zero
            for code, pick in zip(codes, picks):
                value = value + jnp.where(code == count, pick, zero)
            if 8 <= number < 16:
                value = value + jnp.where(own_elem == count, own_pick, zero)
            shared[pair, pl.ds(start + 16 * number, 16), pl.ds(start, ROW)] = value
        rows = pl.ds(0 if place else 384, ROW)
        shared[pair, rows, pl.ds(start, ROW)] = jnp.zeros((ROW, ROW), BF16)

    def moved1_row(extended, level):
        build_weights(extended // 4, extended % 4, 0, level, weights1, (extended - 1) // 2, (extended - 1) % 2)

    def moved2_row(extended, level):
        build_weights(extended // 4, extended % 4, 1, level, weights2, (extended - 3) // 2, (extended - 3) % 2)

    def shared_row(extended):
        build_shared(extended // 4, extended % 4, (extended - 2) // 2, (extended - 2) % 2)

    for copy in local:
        copy.wait()

    for step in range(2):
        prepare(1, step, (0, 1, 2, 3))

    def own_level(level, carry):
        for extended in range(4, 8):
            moved1_row(extended, level)
            moved2_row(extended, level)
        return carry

    lax.fori_loop(0, LEVELS, own_level, 0)
    for extended in range(4, 8):
        shared_row(extended)

    for side in range(2):
        for copy in deps[side]:
            copy.wait_recv()
    prepare(0, 0, (1, 2, 3))
    prepare(2, 0, (0, 1, 2))
    prepare(0, 1, (3,))
    prepare(2, 1, (0,))
    for extended in (2, 3, 8, 9):
        shared_row(extended)

    piece = lax.broadcasted_iota(jnp.int32, (16, BLOCK), 0)
    parts = []
    for slot in range(3):
        whole = masses[slot]
        high = whole.astype(BF16).astype(F32)
        middle = (whole - high).astype(BF16).astype(F32)
        low = whole - high - middle
        mixed = jnp.where(piece == 0, high, jnp.where(piece == 1, middle, jnp.where(piece == 2, low, 0.0)))
        parts.append(mixed.astype(BF16))
    mass_rows = jnp.concatenate(parts, axis=1)
    for pair in range(4):
        begin = ROW + 256 * pair
        total = jnp.dot(mass_rows[:, begin : begin + 512], shared[pair], preferred_element_type=F32)
        inverse[pair] = 1.0 / jnp.sum(total, axis=0, keepdims=True)

    def interpolate(values, table):
        product = jnp.dot(values, table, preferred_element_type=F32)
        low = product[:TRACERS, 256:] + product[TRACERS:, :256] + product[TRACERS:, 256:]
        return product[:TRACERS, :256] + low

    def average(values, pair):
        product = jnp.dot(values, shared[pair], preferred_element_type=F32)
        return (product[:TRACERS] + product[TRACERS:]) * inverse[pair]

    def up_copy():
        return pltpu.make_async_remote_copy(
            src_ref=result.at[0],
            dst_ref=above,
            send_sem=send_up,
            recv_sem=recv_up,
            device_id={"lev": group - 1},
            device_id_type=MESH,
        )

    def one_level(level, carry):
        for extended in (1, 2, 3, 8, 9, 10):
            moved1_row(extended, level)
        for extended in (3, 8):
            moved2_row(extended, level)
        stage0[:, 512:1024] = split(field_own[level])
        for side in range(2):
            field_copy(side, level).wait_recv()
        stage0[:, :512] = split(field_prev[level])
        stage0[:, 1024:] = split(field_next[level])
        for pair in range(5):
            at = 256 * pair
            stage1[:, at : at + 256] = split(interpolate(stage0[:, at : at + 512], weights1[level, pair]))
        for pair in range(4):
            at = 256 * pair
            stage2[:, at : at + 256] = split(average(stage1[:, at : at + 512], pair))
        for pair in range(3):
            at = 256 * pair
            stage3[:, at : at + 256] = split(interpolate(stage2[:, at : at + 512], weights2[level, pair]))
        for pair in range(2):
            at = 256 * pair
            result[level, :, at : at + 256] = average(stage3[:, at : at + 512], pair + 1)

        @pl.when((level == 0) & (group > 0))
        def _():
            up_copy().start()

        return carry

    lax.fori_loop(0, LEVELS, one_level, 0)

    for level in range(LEVELS - 1):
        field = result[level]
        out[level] = field + lifts[pl.ds(level, 1), :] * (result[level + 1] - field)

    for side in range(2):
        for copy in deps[side]:
            copy.wait_send()
        for level in range(LEVELS):
            field_copy(side, level).wait_send()

    last = LEVELS - 1

    @pl.when(group > 0)
    def _():
        up_copy().wait_send()

    @pl.when(group < groups - 1)
    def _():
        up_copy().wait_recv()
        field = result[last]
        out[last] = field + lifts[pl.ds(last, 1), :] * (above[...] - field)

    @pl.when(group == groups - 1)
    def _():
        field = result[last]
        out[last] = field + lifts[pl.ds(last, 1), :] * (field - field)


def local(tracers, owners, source_elements, ref_coords, node_mass, neighbours, lift_fraction):
    dma = pltpu.SemaphoreType.DMA
    return pl.pallas_call(
        kernel,
        out_shape=jax.ShapeDtypeStruct(tracers.shape, F32),
        in_specs=[pl.BlockSpec(memory_space=pltpu.HBM)] * 7,
        out_specs=pl.BlockSpec(memory_space=pltpu.VMEM),
        scratch_shapes=[
            pltpu.VMEM((LEVELS, TRACERS, BLOCK), F32),
            pltpu.VMEM((LEVELS, TRACERS, BLOCK), F32),
            pltpu.VMEM((LEVELS, TRACERS, BLOCK), F32),
            pltpu.VMEM((3, 2, LEVELS, BLOCK), jnp.int32),
            pltpu.VMEM((3, 2, LEVELS, BLOCK), jnp.int32),
            pltpu.VMEM((3, 2, 2, LEVELS, BLOCK), F32),
            pltpu.VMEM((3, 1, BLOCK), F32),
            pltpu.VMEM((3, 3, BLOCK), jnp.int32),
            pltpu.VMEM((LEVELS, BLOCK), F32),
            pltpu.VMEM((3, 2, LEVELS, 3, BLOCK), F32),
            pltpu.VMEM((LEVELS, 5, 512, 512), BF16),
            pltpu.VMEM((LEVELS, 3, 512, 512), BF16),
            pltpu.VMEM((4, 512, 256), BF16),
            pltpu.VMEM((4, 1, 256), F32),
            pltpu.VMEM((2 * TRACERS, 1536), BF16),
            pltpu.VMEM((2 * TRACERS, 1280), BF16),
            pltpu.VMEM((2 * TRACERS, 1024), BF16),
            pltpu.VMEM((2 * TRACERS, 768), BF16),
            pltpu.VMEM((LEVELS, TRACERS, BLOCK), F32),
            pltpu.VMEM((TRACERS, BLOCK), F32),
            dma((7,)),
            dma((2, 8)),
            dma((2, 8)),
            dma((2, LEVELS)),
            dma((2, LEVELS)),
            dma,
            dma,
        ],
        compiler_params=pltpu.CompilerParams(
            collective_id=0, has_side_effects=True, vmem_limit_bytes=32 << 20
        ),
    )(*(pltpu.with_memory_space_constraint(x, pltpu.HBM) for x in (tracers, owners, source_elements, ref_coords, node_mass.reshape(1, -1), neighbours, lift_fraction)))


def solution(mesh):
    in_specs = (
        P("lev", None, "sfc"),
        P(None, "lev", "sfc"),
        P(None, "lev", "sfc"),
        P(None, None, "lev", "sfc"),
        P("sfc"),
        P(None, "sfc"),
        P("lev", "sfc"),
    )
    out_specs = P("lev", None, "sfc")
    return jax.shard_map(local, mesh=mesh, in_specs=in_specs, out_specs=out_specs, check_vma=False)
```

```python
import functools

import jax
import jax.numpy as jnp
from jax import lax
from jax.experimental import pallas as pl
from jax.experimental.pallas import tpu as pltpu
from jax.sharding import PartitionSpec as P

GLL_POINTS = (-1.0, -0.4472135954999579, 0.4472135954999579, 1.0)
MESH = pl.DeviceIdType.MESH
BF16 = jnp.bfloat16
F32 = jnp.float32
LEVELS = 4
TRACERS = 40
ROW = 128
BLOCK = 512


def basis_tables():
    node = lax.broadcasted_iota(jnp.int32, (16, ROW), 0)

    def pick(index, values):
        out = jnp.full((16, ROW), values[3], F32)
        for k in range(3):
            out = jnp.where(index == k, values[k], out)
        return out

    others = [[x for k, x in enumerate(GLL_POINTS) if k != i] for i in range(4)]
    scale = []
    for i in range(4):
        product = 1.0
        for x in others[i]:
            product *= GLL_POINTS[i] - x
        scale.append(1.0 / product)
    first, second = node >> 2, node & 3
    points_a = [pick(first, [others[i][k] for i in range(4)]) for k in range(3)]
    points_b = [pick(second, [others[i][k] for i in range(4)]) for k in range(3)]
    return points_a, points_b, pick(first, scale) * pick(second, scale)


def split(values):
    high = values.astype(BF16).astype(F32)
    return jnp.concatenate([high, values - high], axis=0).astype(BF16)


def spread(row):
    return jnp.broadcast_to(row, (16, ROW))


def kernel(
    tracers, owners, elements, coords, mass, neighbours, lift,
    out,
    field_prev, field_own, field_next, own_ids, elem_ids, refs, masses, copies, lifts, prepared,
    units, shared, inverse, result, above,
    local_sem, send_dep, recv_dep, send_field, recv_field, send_up, recv_up,
):
    me = lax.axis_index("sfc")
    peers = lax.axis_size("sfc")
    group = lax.axis_index("lev")
    groups = lax.axis_size("lev")
    after = lax.rem(me + 1, peers)
    before = lax.rem(me + peers - 1, peers)

    barrier = pltpu.get_barrier_semaphore()
    for device in (before, after):
        pl.semaphore_signal(barrier, inc=1, device_id={"sfc": device}, device_id_type=MESH)

    @pl.when(group < groups - 1)
    def _():
        pl.semaphore_signal(barrier, inc=1, device_id={"lev": group + 1}, device_id_type=MESH)

    local = []

    def fetch(source, target):
        copy = pltpu.make_async_copy(source, target, local_sem.at[len(local)])
        copy.start()
        local.append(copy)

    fetch(owners, own_ids.at[1])
    fetch(elements, elem_ids.at[1])
    fetch(coords, refs.at[1])
    fetch(mass, masses.at[1])
    fetch(neighbours, copies.at[1])
    fetch(lift, lifts)
    fetch(tracers, field_own)

    pl.semaphore_wait(barrier, jnp.where(group > 0, 3, 2))

    sides = ((after, 0, BLOCK - ROW, field_prev), (before, 2, 0, field_next))
    deps = []
    for side, (device, slot, edge, _) in enumerate(sides):
        pieces = (
            (owners.at[0], own_ids.at[slot, 0]),
            (elements.at[0], elem_ids.at[slot, 0]),
            (coords.at[0], refs.at[slot, 0]),
            (mass, masses.at[slot]),
            (neighbours, copies.at[slot]),
            (owners.at[1, :, pl.ds(edge, ROW)], own_ids.at[slot, 1, :, pl.ds(edge, ROW)]),
            (elements.at[1, :, pl.ds(edge, ROW)], elem_ids.at[slot, 1, :, pl.ds(edge, ROW)]),
            (coords.at[1, :, :, pl.ds(edge, ROW)], refs.at[slot, 1, :, :, pl.ds(edge, ROW)]),
        )
        deps.append(
            [
                pltpu.make_async_remote_copy(
                    src_ref=source,
                    dst_ref=target,
                    send_sem=send_dep.at[side, number],
                    recv_sem=recv_dep.at[side, number],
                    device_id={"sfc": device},
                    device_id_type=MESH,
                )
                for number, (source, target) in enumerate(pieces)
            ]
        )
    for pair in zip(*deps):
        for copy in pair:
            copy.start()

    def field_copy(side, level):
        device, _, _, target = sides[side]
        return pltpu.make_async_remote_copy(
            src_ref=tracers.at[level],
            dst_ref=target.at[level],
            send_sem=send_field.at[side, level],
            recv_sem=recv_field.at[side, level],
            device_id={"sfc": device},
            device_id_type=MESH,
        )

    for level in range(LEVELS):
        for side in range(2):
            field_copy(side, level).start()

    points_a, points_b, scale = basis_tables()
    row_mask = 4 * peers - 1
    point_mask = BLOCK * peers - 1
    node = lax.broadcasted_iota(jnp.int32, (16, ROW), 0)
    lane = lax.broadcasted_iota(jnp.int32, (16, ROW), 1)
    zero = jnp.zeros((16, ROW), BF16)
    own_elem = (8 + (lane >> 4)).astype(F32).astype(BF16)
    own_pick = jnp.where((lane & 15) == node, 1.0, 0.0).astype(BF16)

    def prepare(slot, step, rows):
        lanes = pl.ds(rows[0] * ROW, len(rows) * ROW)
        width = len(rows) * ROW
        row = lax.broadcasted_iota(jnp.int32, (LEVELS, width), 1) // ROW + rows[0]
        elem = elem_ids[slot, step, :, lanes]
        source_row = own_ids[slot, step, :, lanes] * 4 + (elem >> 3)
        above_row = (me + (slot - 1)) * 4 - 1 + row
        offset = (source_row - above_row) & row_mask
        code = (offset * 8 + (elem & 7)).astype(F32)
        for level in range(LEVELS):
            prepared[slot, step, level, 0:1, lanes] = code[level : level + 1]
            prepared[slot, step, level, 1:2, lanes] = refs[slot, step, 0, level : level + 1, lanes]
            prepared[slot, step, level, 2:3, lanes] = refs[slot, step, 1, level : level + 1, lanes]

    def build_unit(slot, row, step, level, unit):
        lanes = pl.ds(row * ROW, ROW)
        a = spread(prepared[slot, step, level, 1:2, lanes])
        b = spread(prepared[slot, step, level, 2:3, lanes])
        weight = spread(masses[slot, :, lanes]) * scale
        for point in points_a:
            weight = weight * (a - point)
        for point in points_b:
            weight = weight * (b - point)
        high = weight.astype(BF16)
        units[level, unit, 0] = spread(prepared[slot, step, level, 0:1, lanes]).astype(BF16)
        units[level, unit, 1] = high
        units[level, unit, 2] = (weight - high.astype(F32)).astype(BF16)

    def build_shared(slot, row, place):
        lanes = pl.ds(row * ROW, ROW)
        first = ((me + (slot - 1)) * 4 + (row - 1)) * ROW
        codes, picks = [], []
        for number in range(3):
            copy = copies[slot, pl.ds(number, 1), lanes]
            offset = (copy - first) & point_mask
            code = jnp.where(copy >= 0, offset >> 4, -1)
            codes.append(spread(code.astype(F32)).astype(BF16))
            picks.append(jnp.where(spread(offset & 15) == node, 1.0, 0.0).astype(BF16))
        for number in range(24):
            count = jnp.asarray(number, BF16)
            value = None
            for code, pick in zip(codes, picks):
                term = jnp.where(code == count, pick, zero)
                value = term if value is None else value + term
            if 8 <= number < 16:
                value = value + jnp.where(own_elem == count, own_pick, zero)
            shared[place, pl.ds(16 * number, 16), :] = value

    def moved1_row(extended, level):
        build_unit(extended // 4, extended % 4, 0, level, extended - 1)

    def moved2_row(extended, level):
        build_unit(extended // 4, extended % 4, 1, level, 7 + extended)

    def shared_row(extended):
        build_shared(extended // 4, extended % 4, extended - 2)

    for copy in local:
        copy.wait()

    for step in range(2):
        prepare(1, step, (0, 1, 2, 3))

    def own_level(level, carry):
        for extended in range(4, 8):
            moved1_row(extended, level)
            moved2_row(extended, level)
        return carry

    lax.fori_loop(0, LEVELS, own_level, 0)
    for extended in range(4, 8):
        shared_row(extended)

    for side in range(2):
        for copy in deps[side]:
            copy.wait_recv()
    prepare(0, 0, (1, 2, 3))
    prepare(2, 0, (0, 1, 2))
    prepare(0, 1, (3,))
    prepare(2, 1, (0,))
    for extended in (2, 3, 8, 9):
        shared_row(extended)

    piece = lax.broadcasted_iota(jnp.int32, (16, BLOCK), 0)
    parts = []
    for slot in range(3):
        whole = masses[slot]
        high = whole.astype(BF16).astype(F32)
        middle = (whole - high).astype(BF16).astype(F32)
        low = whole - high - middle
        mixed = jnp.where(piece == 0, high, jnp.where(piece == 1, middle, jnp.where(piece == 2, low, 0.0)))
        parts.append(mixed.astype(BF16))
    mass_rows = jnp.concatenate(parts, axis=1)
    blank = jnp.zeros((ROW, ROW), BF16)

    def shared_pair(pair):
        first = jnp.concatenate([shared[2 * pair], blank], axis=0)
        second = jnp.concatenate([blank, shared[2 * pair + 1]], axis=0)
        return jnp.concatenate([first, second], axis=1)

    for pair in range(4):
        begin = ROW + 256 * pair
        total = jnp.dot(mass_rows[:, begin : begin + 512], shared_pair(pair), preferred_element_type=F32)
        inverse[pair] = 1.0 / jnp.sum(total, axis=0, keepdims=True)

    def interpolate(rows, level, unit):
        code, high, low = (units[level, unit, part] for part in range(3))
        hits = [code == jnp.asarray(number, BF16) for number in range(24)]
        table = jnp.concatenate(
            [
                jnp.concatenate([jnp.where(hit, part, zero) for hit in hits], axis=0)
                for part in (high, low)
            ],
            axis=1,
        )
        product = jnp.dot(jnp.concatenate(rows, axis=1), table, preferred_element_type=F32)
        low = product[:TRACERS, ROW:] + product[TRACERS:, :ROW] + product[TRACERS:, ROW:]
        return split(product[:TRACERS, :ROW] + low)

    def average(rows, pair):
        product = jnp.dot(jnp.concatenate(rows, axis=1), shared_pair(pair), preferred_element_type=F32)
        return (product[:TRACERS] + product[TRACERS:]) * inverse[pair]

    def up_copy():
        return pltpu.make_async_remote_copy(
            src_ref=result.at[0],
            dst_ref=above,
            send_sem=send_up,
            recv_sem=recv_up,
            device_id={"lev": group - 1},
            device_id_type=MESH,
        )

    def one_level(level, carry):
        for extended in (1, 2, 3, 8, 9, 10):
            moved1_row(extended, level)
        for extended in (3, 8):
            moved2_row(extended, level)
        for side in range(2):
            field_copy(side, level).wait_recv()
        rows = {}
        for slot, block in enumerate((field_prev, field_own, field_next)):
            for row in range(4):
                rows[4 * slot + row] = split(block[level, :, ROW * row : ROW * (row + 1)])
        moved = {e: interpolate([rows[e + k] for k in (-1, 0, 1)], level, e - 1) for e in range(1, 11)}
        rows = {}
        for pair in range(4):
            e = 2 + 2 * pair
            both = split(average([moved[e + k] for k in (-1, 0, 1, 2)], pair))
            rows[e], rows[e + 1] = both[:, :ROW], both[:, ROW:]
        moved = {e: interpolate([rows[e + k] for k in (-1, 0, 1)], level, e + 7) for e in range(3, 9)}
        for pair in (1, 2):
            e = 2 + 2 * pair
            at = 256 * (pair - 1)
            result[level, :, at : at + 256] = average([moved[e + k] for k in (-1, 0, 1, 2)], pair)

        @pl.when((level == 0) & (group > 0))
        def _():
            up_copy().start()

        return carry

    lax.fori_loop(0, LEVELS, one_level, 0)

    for level in range(LEVELS - 1):
        field = result[level]
        out[level] = field + lifts[pl.ds(level, 1), :] * (result[level + 1] - field)

    for side in range(2):
        for copy in deps[side]:
            copy.wait_send()
        for level in range(LEVELS):
            field_copy(side, level).wait_send()

    last = LEVELS - 1

    @pl.when(group > 0)
    def _():
        up_copy().wait_send()

    @pl.when(group < groups - 1)
    def _():
        up_copy().wait_recv()
        field = result[last]
        out[last] = field + lifts[pl.ds(last, 1), :] * (above[...] - field)

    @pl.when(group == groups - 1)
    def _():
        field = result[last]
        out[last] = field + lifts[pl.ds(last, 1), :] * (field - field)


def local(tracers, owners, source_elements, ref_coords, node_mass, neighbours, lift_fraction):
    dma = pltpu.SemaphoreType.DMA
    return pl.pallas_call(
        kernel,
        out_shape=jax.ShapeDtypeStruct(tracers.shape, F32),
        in_specs=[pl.BlockSpec(memory_space=pltpu.HBM)] * 7,
        out_specs=pl.BlockSpec(memory_space=pltpu.VMEM),
        scratch_shapes=[
            pltpu.VMEM((LEVELS, TRACERS, BLOCK), F32),
            pltpu.VMEM((LEVELS, TRACERS, BLOCK), F32),
            pltpu.VMEM((LEVELS, TRACERS, BLOCK), F32),
            pltpu.VMEM((3, 2, LEVELS, BLOCK), jnp.int32),
            pltpu.VMEM((3, 2, LEVELS, BLOCK), jnp.int32),
            pltpu.VMEM((3, 2, 2, LEVELS, BLOCK), F32),
            pltpu.VMEM((3, 1, BLOCK), F32),
            pltpu.VMEM((3, 3, BLOCK), jnp.int32),
            pltpu.VMEM((LEVELS, BLOCK), F32),
            pltpu.VMEM((3, 2, LEVELS, 3, BLOCK), F32),
            pltpu.VMEM((LEVELS, 16, 3, 16, ROW), BF16),
            pltpu.VMEM((8, 384, ROW), BF16),
            pltpu.VMEM((4, 1, 256), F32),
            pltpu.VMEM((LEVELS, TRACERS, BLOCK), F32),
            pltpu.VMEM((TRACERS, BLOCK), F32),
            dma((7,)),
            dma((2, 8)),
            dma((2, 8)),
            dma((2, LEVELS)),
            dma((2, LEVELS)),
            dma,
            dma,
        ],
        compiler_params=pltpu.CompilerParams(
            collective_id=0, has_side_effects=True, vmem_limit_bytes=32 << 20
        ),
    )(*(pltpu.with_memory_space_constraint(x, pltpu.HBM) for x in (tracers, owners, source_elements, ref_coords, node_mass.reshape(1, -1), neighbours, lift_fraction)))


def solution(mesh):
    in_specs = (
        P("lev", None, "sfc"),
        P(None, "lev", "sfc"),
        P(None, "lev", "sfc"),
        P(None, None, "lev", "sfc"),
        P("sfc"),
        P(None, "sfc"),
        P("lev", "sfc"),
    )
    out_specs = P("lev", None, "sfc")
    return jax.shard_map(local, mesh=mesh, in_specs=in_specs, out_specs=out_specs, check_vma=False)
```

```python
import functools

import jax
import jax.numpy as jnp
from jax import lax
from jax.experimental import pallas as pl
from jax.experimental.pallas import tpu as pltpu
from jax.sharding import PartitionSpec as P

GLL_POINTS = (-1.0, -0.4472135954999579, 0.4472135954999579, 1.0)
MESH = pl.DeviceIdType.MESH
BF16 = jnp.bfloat16
F32 = jnp.float32
LEVELS = 4
TRACERS = 40
ROW = 128
BLOCK = 512


def basis_tables():
    node = lax.broadcasted_iota(jnp.int32, (16, ROW), 0)

    def pick(index, values):
        out = jnp.full((16, ROW), values[3], F32)
        for k in range(3):
            out = jnp.where(index == k, values[k], out)
        return out

    others = [[x for k, x in enumerate(GLL_POINTS) if k != i] for i in range(4)]
    scale = []
    for i in range(4):
        product = 1.0
        for x in others[i]:
            product *= GLL_POINTS[i] - x
        scale.append(1.0 / product)
    first, second = node >> 2, node & 3
    points_a = [pick(first, [others[i][k] for i in range(4)]) for k in range(3)]
    points_b = [pick(second, [others[i][k] for i in range(4)]) for k in range(3)]
    return points_a, points_b, pick(first, scale) * pick(second, scale)


def split(values):
    high = values.astype(BF16).astype(F32)
    return jnp.concatenate([high, values - high], axis=0).astype(BF16)


def spread(row):
    return jnp.broadcast_to(row, (16, ROW))


def kernel(
    tracers, owners, elements, coords, mass, neighbours, lift,
    out,
    fields, own_ids, elem_ids, refs, masses, copies, lifts, prepared,
    units, shared, inverse, rows0, moved1, rows1, moved2, result, above,
    local_sem, send_dep, recv_dep, send_field, recv_field, send_up, recv_up,
):
    me = lax.axis_index("sfc")
    peers = lax.axis_size("sfc")
    group = lax.axis_index("lev")
    groups = lax.axis_size("lev")
    after = lax.rem(me + 1, peers)
    before = lax.rem(me + peers - 1, peers)

    barrier = pltpu.get_barrier_semaphore()
    for device in (before, after):
        pl.semaphore_signal(barrier, inc=1, device_id={"sfc": device}, device_id_type=MESH)

    @pl.when(group < groups - 1)
    def _():
        pl.semaphore_signal(barrier, inc=1, device_id={"lev": group + 1}, device_id_type=MESH)

    local = []

    def fetch(source, target):
        copy = pltpu.make_async_copy(source, target, local_sem.at[len(local)])
        copy.start()
        local.append(copy)

    fetch(owners, own_ids.at[1])
    fetch(elements, elem_ids.at[1])
    fetch(coords, refs.at[1])
    fetch(mass, masses.at[1])
    fetch(neighbours, copies.at[1])
    fetch(lift, lifts)
    fetch(tracers, fields.at[1])

    pl.semaphore_wait(barrier, jnp.where(group > 0, 3, 2))

    odd = lax.rem(me, 2)
    far, near = 0, 1
    device = (jnp.where(odd == 1, after, before), jnp.where(odd == 1, before, after))
    slot_here = (2 * odd, 2 - 2 * odd)
    slot_there = (2 - 2 * odd, 2 * odd)

    def dep_copies(side, slot):
        three = pl.ds(pl.multiple_of((2 - slot) * 64, ROW), BLOCK - ROW)
        one = pl.ds(pl.multiple_of((2 - slot) * 192, ROW), ROW)
        pieces = (
            (owners.at[0, :, three], own_ids.at[slot, 0, :, three]),
            (elements.at[0, :, three], elem_ids.at[slot, 0, :, three]),
            (coords.at[0, :, :, three], refs.at[slot, 0, :, :, three]),
            (mass, masses.at[slot]),
            (neighbours, copies.at[slot]),
            (owners.at[1, :, one], own_ids.at[slot, 1, :, one]),
            (elements.at[1, :, one], elem_ids.at[slot, 1, :, one]),
            (coords.at[1, :, :, one], refs.at[slot, 1, :, :, one]),
        )
        return [
            pltpu.make_async_remote_copy(
                src_ref=source,
                dst_ref=target,
                send_sem=send_dep.at[side, number],
                recv_sem=recv_dep.at[side, number],
                device_id={"sfc": device[side]},
                device_id_type=MESH,
            )
            for number, (source, target) in enumerate(pieces)
        ]

    def field_copy(side, slot, level):
        return pltpu.make_async_remote_copy(
            src_ref=tracers.at[level],
            dst_ref=fields.at[slot, level],
            send_sem=send_field.at[side, level],
            recv_sem=recv_field.at[side, level],
            device_id={"sfc": device[side]},
            device_id_type=MESH,
        )

    for side in (far, near):
        for copy in dep_copies(side, slot_there[side]):
            copy.start()
    for level in range(LEVELS):
        for side in (far, near):
            field_copy(side, slot_there[side], level).start()

    points_a, points_b, scale = basis_tables()
    row_mask = 4 * peers - 1
    point_mask = BLOCK * peers - 1
    node = lax.broadcasted_iota(jnp.int32, (16, ROW), 0)
    lane = lax.broadcasted_iota(jnp.int32, (16, ROW), 1)
    zero = jnp.zeros((16, ROW), BF16)
    own_elem = (8 + (lane >> 4)).astype(F32).astype(BF16)
    own_pick = jnp.where((lane & 15) == node, 1.0, 0.0).astype(BF16)

    def prepare(slot, step, start, count):
        width = count * ROW
        lanes = pl.ds(pl.multiple_of(start * ROW, ROW), width)
        row = lax.broadcasted_iota(jnp.int32, (LEVELS, width), 1) // ROW + start
        elem = elem_ids[slot, step, :, lanes]
        source_row = own_ids[slot, step, :, lanes] * 4 + (elem >> 3)
        above_row = (me + (slot - 1)) * 4 - 1 + row
        offset = (source_row - above_row) & row_mask
        code = (offset * 8 + (elem & 7)).astype(F32)
        first, second = refs[slot, step, 0, :, lanes], refs[slot, step, 1, :, lanes]
        for level in range(LEVELS):
            prepared[slot, step, level, 0:1, lanes] = code[level : level + 1]
            prepared[slot, step, level, 1:2, lanes] = first[level : level + 1]
            prepared[slot, step, level, 2:3, lanes] = second[level : level + 1]

    def build_unit(slot, row, step, level, unit):
        lanes = pl.ds(pl.multiple_of(row * ROW, ROW), ROW)
        a = spread(prepared[slot, step, level, 1:2, lanes])
        b = spread(prepared[slot, step, level, 2:3, lanes])
        weight = spread(masses[slot, :, lanes]) * scale
        for point in points_a:
            weight = weight * (a - point)
        for point in points_b:
            weight = weight * (b - point)
        high = weight.astype(BF16).astype(F32)
        units[level, unit, 0] = spread(prepared[slot, step, level, 0:1, lanes])
        units[level, unit, 1] = high
        units[level, unit, 2] = weight - high

    def build_shared(slot, row, place):
        lanes = pl.ds(pl.multiple_of(row * ROW, ROW), ROW)
        first = ((me + (slot - 1)) * 4 + (row - 1)) * ROW
        codes, picks = [], []
        for number in range(3):
            copy = copies[slot, pl.ds(number, 1), lanes]
            offset = (copy - first) & point_mask
            code = jnp.where(copy >= 0, offset >> 4, -1)
            codes.append(spread(code.astype(F32)).astype(BF16))
            picks.append(jnp.where(spread(offset & 15) == node, 1.0, 0.0).astype(BF16))
        for number in range(24):
            count = jnp.asarray(number, BF16)
            value = None
            for code, pick in zip(codes, picks):
                term = jnp.where(code == count, pick, zero)
                value = term if value is None else value + term
            if 8 <= number < 16:
                value = value + jnp.where(own_elem == count, own_pick, zero)
            shared[place, pl.ds(16 * number, 16), :] = value

    def moved1_unit(slot, row, level):
        build_unit(slot, row, 0, level, 4 * slot + row - 1)

    def moved2_unit(slot, row, level):
        build_unit(slot, row, 1, level, 4 * slot + row + 7)

    for copy in local:
        copy.wait()
    for step in range(2):
        prepare(1, step, 0, 4)

    def own_level(level, carry):
        for row in range(4):
            moved1_unit(1, row, level)
            moved2_unit(1, row, level)
            rows0[level, 4 + row] = split(fields[1, level, :, ROW * row : ROW * (row + 1)])
        return carry

    lax.fori_loop(0, LEVELS, own_level, 0)
    for row in range(4):
        build_shared(1, row, 2 + row)

    blank = jnp.zeros((ROW, ROW), BF16)

    def shared_pair(pair):
        first = jnp.concatenate([shared[2 * pair], blank], axis=0)
        second = jnp.concatenate([blank, shared[2 * pair + 1]], axis=0)
        return jnp.concatenate([first, second], axis=1)

    piece = lax.broadcasted_iota(jnp.int32, (16, ROW), 0)

    def mass_rows(extended):
        lanes = pl.ds(pl.multiple_of((extended % 4) * ROW, ROW), ROW)
        whole = spread(masses[extended // 4, :, lanes])
        high = whole.astype(BF16).astype(F32)
        middle = (whole - high).astype(BF16).astype(F32)
        low = whole - high - middle
        mixed = jnp.where(piece == 0, high, jnp.where(piece == 1, middle, jnp.where(piece == 2, low, 0.0)))
        return mixed.astype(BF16)

    def invert_masses(pair):
        parts = jnp.concatenate([mass_rows(2 * pair + 1 + k) for k in range(4)], axis=1)
        total = jnp.dot(parts, shared_pair(pair), preferred_element_type=F32)
        inverse[pair] = 1.0 / jnp.sum(total, axis=0, keepdims=True)

    def interpolate(source, level, extended, unit):
        code, high, low = (units[level, unit, part].astype(BF16) for part in range(3))
        hits = [code == jnp.asarray(number, BF16) for number in range(24)]
        table = jnp.concatenate(
            [
                jnp.concatenate([jnp.where(hit, part, zero) for hit in hits], axis=0)
                for part in (high, low)
            ],
            axis=1,
        )
        three = source[level, pl.ds(extended - 1, 3)]
        rows = jnp.concatenate([three[k] for k in range(3)], axis=1)
        product = jnp.dot(rows, table, preferred_element_type=F32)
        low = product[:TRACERS, ROW:] + product[TRACERS:, :ROW] + product[TRACERS:, ROW:]
        return product[:TRACERS, :ROW] + low

    def average(source, level, pair):
        four = source[level, pl.ds(2 * pair + 1, 4)]
        rows = jnp.concatenate([four[k] for k in range(4)], axis=1)
        product = jnp.dot(rows, shared_pair(pair), preferred_element_type=F32)
        return (product[:TRACERS] + product[TRACERS:]) * inverse[pair]

    def up_copy():
        return pltpu.make_async_remote_copy(
            src_ref=result.at[0],
            dst_ref=above,
            send_sem=send_up,
            recv_sem=recv_up,
            device_id={"lev": group - 1},
            device_id_type=MESH,
        )

    def first_part(side):
        slot = slot_here[side]
        for copy in dep_copies(side, slot):
            copy.wait_recv()
        inner = 3 - 3 * (slot // 2)
        prepare(slot, 0, 1 - slot // 2, 3)
        prepare(slot, 1, inner, 1)
        pair = 3 * (slot // 2)
        for k in range(2):
            extended = 2 + 2 * pair + k
            build_shared(slot, extended % 4, extended - 2)
        for k in range(2):
            invert_masses(2 * (slot // 2) + k)

    def arrived(side, level):
        slot = slot_here[side]
        for k in range(3):
            moved1_unit(slot, 1 - slot // 2 + k, level)
        moved2_unit(slot, 3 - 3 * (slot // 2), level)
        field_copy(side, slot, level).wait_recv()
        for row in range(4):
            rows0[level, 4 * slot + row] = split(fields[slot, level, :, ROW * row : ROW * (row + 1)])

    def step(level, start1, count1, pairs, start2, count2):
        for k in range(count1):
            moved1[level, start1 + k] = split(interpolate(rows0, level, start1 + k, start1 + k - 1))
        for k in range(2):
            both = split(average(moved1, level, pairs + k))
            rows1[level, 2 + 2 * (pairs + k)] = both[:, :ROW]
            rows1[level, 3 + 2 * (pairs + k)] = both[:, ROW:]
        for k in range(count2):
            moved2[level, start2 + k] = split(interpolate(rows1, level, start2 + k, start2 + k + 7))

    def near_arrivals(half, carry):
        for k in range(2):
            arrived(near, 2 * half + k)
        for k in range(2):
            for row in range(6):
                level, extended = 2 * half + k, 5 - 4 * odd + row
                moved1[level, extended] = split(interpolate(rows0, level, extended, extended - 1))
        return carry

    def near_rest():
        for k in range(2):
            pair = 2 - 2 * odd + k
            levels = [moved1[level, pl.ds(2 * pair + 1, 4)] for level in range(LEVELS)]
            rows = jnp.concatenate([jnp.concatenate([four[j] for j in range(4)], axis=1) for four in levels], axis=0)
            product = jnp.dot(rows, shared_pair(pair), preferred_element_type=F32)
            for level in range(LEVELS):
                high = product[2 * TRACERS * level : 2 * TRACERS * level + TRACERS]
                low = product[2 * TRACERS * level + TRACERS : 2 * TRACERS * (level + 1)]
                both = split((high + low) * inverse[pair])
                rows1[level, 2 + 2 * pair] = both[:, :ROW]
                rows1[level, 3 + 2 * pair] = both[:, ROW:]
        for level in range(LEVELS):
            for k in range(2):
                extended = 7 - 4 * odd + k
                moved2[level, extended] = split(interpolate(rows1, level, extended, extended + 7))

    def far_level(level, carry):
        arrived(far, level)
        step(level, 1 + 6 * odd, 4, 2 * odd, 3 + 2 * odd, 4)
        for pair in (1, 2):
            at = 256 * (pair - 1)
            result[level, :, at : at + 256] = average(moved2, level, pair)

        @pl.when((level == 0) & (group > 0))
        def _():
            up_copy().start()

        return carry

    first_part(near)
    lax.fori_loop(0, LEVELS // 2, near_arrivals, 0)
    near_rest()
    first_part(far)
    lax.fori_loop(0, LEVELS, far_level, 0)

    for level in range(LEVELS - 1):
        field = result[level]
        out[level] = field + lifts[pl.ds(level, 1), :] * (result[level + 1] - field)

    for side in (far, near):
        for copy in dep_copies(side, slot_there[side]):
            copy.wait_send()
        for level in range(LEVELS):
            field_copy(side, slot_there[side], level).wait_send()

    last = LEVELS - 1

    @pl.when(group > 0)
    def _():
        up_copy().wait_send()

    @pl.when(group < groups - 1)
    def _():
        up_copy().wait_recv()
        field = result[last]
        out[last] = field + lifts[pl.ds(last, 1), :] * (above[...] - field)

    @pl.when(group == groups - 1)
    def _():
        field = result[last]
        out[last] = field + lifts[pl.ds(last, 1), :] * (field - field)


def local(tracers, owners, source_elements, ref_coords, node_mass, neighbours, lift_fraction):
    dma = pltpu.SemaphoreType.DMA
    return pl.pallas_call(
        kernel,
        out_shape=jax.ShapeDtypeStruct(tracers.shape, F32),
        in_specs=[pl.BlockSpec(memory_space=pltpu.HBM)] * 7,
        out_specs=pl.BlockSpec(memory_space=pltpu.VMEM),
        scratch_shapes=[
            pltpu.VMEM((3, LEVELS, TRACERS, BLOCK), F32),
            pltpu.VMEM((3, 2, LEVELS, BLOCK), jnp.int32),
            pltpu.VMEM((3, 2, LEVELS, BLOCK), jnp.int32),
            pltpu.VMEM((3, 2, 2, LEVELS, BLOCK), F32),
            pltpu.VMEM((3, 1, BLOCK), F32),
            pltpu.VMEM((3, 3, BLOCK), jnp.int32),
            pltpu.VMEM((LEVELS, BLOCK), F32),
            pltpu.VMEM((3, 2, LEVELS, 3, BLOCK), F32),
            pltpu.VMEM((LEVELS, 16, 3, 16, ROW), F32),
            pltpu.VMEM((8, 384, ROW), BF16),
            pltpu.VMEM((4, 1, 256), F32),
            pltpu.VMEM((LEVELS, 12, 2 * TRACERS, ROW), BF16),
            pltpu.VMEM((LEVELS, 12, 2 * TRACERS, ROW), BF16),
            pltpu.VMEM((LEVELS, 12, 2 * TRACERS, ROW), BF16),
            pltpu.VMEM((LEVELS, 12, 2 * TRACERS, ROW), BF16),
            pltpu.VMEM((LEVELS, TRACERS, BLOCK), F32),
            pltpu.VMEM((TRACERS, BLOCK), F32),
            dma((7,)),
            dma((2, 8)),
            dma((2, 8)),
            dma((2, LEVELS)),
            dma((2, LEVELS)),
            dma,
            dma,
        ],
        compiler_params=pltpu.CompilerParams(
            collective_id=0, has_side_effects=True, vmem_limit_bytes=32 << 20
        ),
    )(*(pltpu.with_memory_space_constraint(x, pltpu.HBM) for x in (tracers, owners, source_elements, ref_coords, node_mass.reshape(1, -1), neighbours, lift_fraction)))


def solution(mesh):
    in_specs = (
        P("lev", None, "sfc"),
        P(None, "lev", "sfc"),
        P(None, "lev", "sfc"),
        P(None, None, "lev", "sfc"),
        P("sfc"),
        P(None, "sfc"),
        P("lev", "sfc"),
    )
    out_specs = P("lev", None, "sfc")
    return jax.shard_map(local, mesh=mesh, in_specs=in_specs, out_specs=out_specs, check_vma=False)
```

```python
import functools

import jax
import jax.numpy as jnp
from jax import lax
from jax.experimental import pallas as pl
from jax.experimental.pallas import tpu as pltpu
from jax.sharding import PartitionSpec as P

GLL_POINTS = (-1.0, -0.4472135954999579, 0.4472135954999579, 1.0)
MESH = pl.DeviceIdType.MESH
BF16 = jnp.bfloat16
F32 = jnp.float32
LEVELS = 4
TRACERS = 40
ROW = 128
BLOCK = 512


def basis_tables():
    node = lax.broadcasted_iota(jnp.int32, (16, ROW), 0)

    def pick(index, values):
        out = jnp.full((16, ROW), values[3], F32)
        for k in range(3):
            out = jnp.where(index == k, values[k], out)
        return out

    others = [[x for k, x in enumerate(GLL_POINTS) if k != i] for i in range(4)]
    scale = []
    for i in range(4):
        product = 1.0
        for x in others[i]:
            product *= GLL_POINTS[i] - x
        scale.append(1.0 / product)
    first, second = node >> 2, node & 3
    points_a = [pick(first, [others[i][k] for i in range(4)]) for k in range(3)]
    points_b = [pick(second, [others[i][k] for i in range(4)]) for k in range(3)]
    return points_a, points_b, pick(first, scale) * pick(second, scale)


def split(values):
    high = values.astype(BF16).astype(F32)
    return jnp.concatenate([high, values - high], axis=0).astype(BF16)


def spread(row):
    return jnp.broadcast_to(row, (16, ROW))


def kernel(
    tracers, owners, elements, coords, mass, neighbours, lift,
    out,
    fields, own_ids, elem_ids, refs, masses, copies, lifts, prepared,
    units, shared, inverse, rows0, moved1, rows1, moved2, result, above,
    local_sem, send_dep, recv_dep, send_field, recv_field, send_up, recv_up,
):
    me = lax.axis_index("sfc")
    peers = lax.axis_size("sfc")
    group = lax.axis_index("lev")
    groups = lax.axis_size("lev")
    after = lax.rem(me + 1, peers)
    before = lax.rem(me + peers - 1, peers)

    odd = lax.rem(me, 2)
    far, near = 0, 1
    device = (jnp.where(odd == 1, after, before), jnp.where(odd == 1, before, after))
    slot_here = (2 * odd, 2 - 2 * odd)
    slot_there = (2 - 2 * odd, 2 * odd)

    first, last = me == 0, me == peers - 1

    barrier = pltpu.get_barrier_semaphore()
    pl.semaphore_signal(barrier, inc=1, device_id={"sfc": device[near]}, device_id_type=MESH)

    @pl.when(jnp.logical_not(last))
    def _():
        pl.semaphore_signal(barrier, inc=1, device_id={"sfc": device[far]}, device_id_type=MESH)

    @pl.when(group < groups - 1)
    def _():
        pl.semaphore_signal(barrier, inc=1, device_id={"lev": group + 1}, device_id_type=MESH)

    local = []

    def fetch(source, target):
        copy = pltpu.make_async_copy(source, target, local_sem.at[len(local)])
        copy.start()
        local.append(copy)

    fetch(owners, own_ids.at[1])
    fetch(elements, elem_ids.at[1])
    fetch(coords, refs.at[1])
    fetch(mass, masses.at[1])
    fetch(neighbours, copies.at[1])
    fetch(lift, lifts)
    fetch(tracers, fields.at[1])

    pl.semaphore_wait(barrier, 1 + jnp.where(first, 0, 1) + jnp.where(group > 0, 1, 0))

    def dep_copies(side, slot):
        three = pl.ds(pl.multiple_of((2 - slot) * 64, ROW), BLOCK - ROW)
        one = pl.ds(pl.multiple_of((2 - slot) * 192, ROW), ROW)
        pieces = (
            (owners.at[0, :, three], own_ids.at[slot, 0, :, three]),
            (elements.at[0, :, three], elem_ids.at[slot, 0, :, three]),
            (coords.at[0, :, :, three], refs.at[slot, 0, :, :, three]),
            (mass, masses.at[slot]),
            (neighbours, copies.at[slot]),
            (owners.at[1, :, one], own_ids.at[slot, 1, :, one]),
            (elements.at[1, :, one], elem_ids.at[slot, 1, :, one]),
            (coords.at[1, :, :, one], refs.at[slot, 1, :, :, one]),
        )
        return [
            pltpu.make_async_remote_copy(
                src_ref=source,
                dst_ref=target,
                send_sem=send_dep.at[side, number],
                recv_sem=recv_dep.at[side, number],
                device_id={"sfc": device[side]},
                device_id_type=MESH,
            )
            for number, (source, target) in enumerate(pieces)
        ]

    def field_copy(side, slot, level):
        return pltpu.make_async_remote_copy(
            src_ref=tracers.at[level],
            dst_ref=fields.at[slot, level],
            send_sem=send_field.at[side, level],
            recv_sem=recv_field.at[side, level],
            device_id={"sfc": device[side]},
            device_id_type=MESH,
        )

    def send(side):
        for copy in dep_copies(side, slot_there[side]):
            copy.start()
        for level in range(LEVELS):
            field_copy(side, slot_there[side], level).start()

    @pl.when(jnp.logical_not(first))
    def _():
        send(far)

    send(near)

    points_a, points_b, scale = basis_tables()
    row_mask = 4 * peers - 1
    point_mask = BLOCK * peers - 1
    node = lax.broadcasted_iota(jnp.int32, (16, ROW), 0)
    lane = lax.broadcasted_iota(jnp.int32, (16, ROW), 1)
    zero = jnp.zeros((16, ROW), BF16)
    own_elem = (8 + (lane >> 4)).astype(F32).astype(BF16)
    own_pick = jnp.where((lane & 15) == node, 1.0, 0.0).astype(BF16)

    def prepare(slot, step, start, count):
        width = count * ROW
        lanes = pl.ds(pl.multiple_of(start * ROW, ROW), width)
        row = lax.broadcasted_iota(jnp.int32, (LEVELS, width), 1) // ROW + start
        elem = elem_ids[slot, step, :, lanes]
        source_row = own_ids[slot, step, :, lanes] * 4 + (elem >> 3)
        above_row = (me + (slot - 1)) * 4 - 1 + row
        offset = (source_row - above_row) & row_mask
        code = (offset * 8 + (elem & 7)).astype(F32)
        first, second = refs[slot, step, 0, :, lanes], refs[slot, step, 1, :, lanes]
        for level in range(LEVELS):
            prepared[slot, step, level, 0:1, lanes] = code[level : level + 1]
            prepared[slot, step, level, 1:2, lanes] = first[level : level + 1]
            prepared[slot, step, level, 2:3, lanes] = second[level : level + 1]

    def build_unit(slot, row, step, level, unit):
        lanes = pl.ds(pl.multiple_of(row * ROW, ROW), ROW)
        a = spread(prepared[slot, step, level, 1:2, lanes])
        b = spread(prepared[slot, step, level, 2:3, lanes])
        weight = spread(masses[slot, :, lanes]) * scale
        for point in points_a:
            weight = weight * (a - point)
        for point in points_b:
            weight = weight * (b - point)
        high = weight.astype(BF16).astype(F32)
        units[level, unit, 0] = spread(prepared[slot, step, level, 0:1, lanes])
        units[level, unit, 1] = high
        units[level, unit, 2] = weight - high

    def build_shared(slot, row, place):
        lanes = pl.ds(pl.multiple_of(row * ROW, ROW), ROW)
        first = ((me + (slot - 1)) * 4 + (row - 1)) * ROW
        codes, picks = [], []
        for number in range(3):
            copy = copies[slot, pl.ds(number, 1), lanes]
            offset = (copy - first) & point_mask
            code = jnp.where(copy >= 0, offset >> 4, -1)
            codes.append(spread(code.astype(F32)).astype(BF16))
            picks.append(jnp.where(spread(offset & 15) == node, 1.0, 0.0).astype(BF16))
        for number in range(24):
            count = jnp.asarray(number, BF16)
            value = None
            for code, pick in zip(codes, picks):
                term = jnp.where(code == count, pick, zero)
                value = term if value is None else value + term
            if 8 <= number < 16:
                value = value + jnp.where(own_elem == count, own_pick, zero)
            shared[place, pl.ds(16 * number, 16), :] = value

    def moved1_unit(slot, row, level):
        build_unit(slot, row, 0, level, 4 * slot + row - 1)

    def moved2_unit(slot, row, level):
        build_unit(slot, row, 1, level, 4 * slot + row + 7)

    for copy in local:
        copy.wait()
    for step in range(2):
        prepare(1, step, 0, 4)

    def own_level(level, carry):
        for row in range(4):
            moved1_unit(1, row, level)
            moved2_unit(1, row, level)
            rows0[level, 4 + row] = split(fields[1, level, :, ROW * row : ROW * (row + 1)])
        return carry

    lax.fori_loop(0, LEVELS, own_level, 0)
    for row in range(4):
        build_shared(1, row, 2 + row)

    blank = jnp.zeros((ROW, ROW), BF16)

    def shared_pair(pair):
        first = jnp.concatenate([shared[2 * pair], blank], axis=0)
        second = jnp.concatenate([blank, shared[2 * pair + 1]], axis=0)
        return jnp.concatenate([first, second], axis=1)

    piece = lax.broadcasted_iota(jnp.int32, (16, ROW), 0)

    def mass_rows(extended):
        lanes = pl.ds(pl.multiple_of((extended % 4) * ROW, ROW), ROW)
        whole = spread(masses[extended // 4, :, lanes])
        high = whole.astype(BF16).astype(F32)
        middle = (whole - high).astype(BF16).astype(F32)
        low = whole - high - middle
        mixed = jnp.where(piece == 0, high, jnp.where(piece == 1, middle, jnp.where(piece == 2, low, 0.0)))
        return mixed.astype(BF16)

    def invert_masses(pair):
        parts = jnp.concatenate([mass_rows(2 * pair + 1 + k) for k in range(4)], axis=1)
        total = jnp.dot(parts, shared_pair(pair), preferred_element_type=F32)
        inverse[pair] = 1.0 / jnp.sum(total, axis=0, keepdims=True)

    def interpolate(source, level, extended, unit):
        code, high, low = (units[level, unit, part].astype(BF16) for part in range(3))
        hits = [code == jnp.asarray(number, BF16) for number in range(24)]
        table = jnp.concatenate(
            [
                jnp.concatenate([jnp.where(hit, part, zero) for hit in hits], axis=0)
                for part in (high, low)
            ],
            axis=1,
        )
        three = source[level, pl.ds(extended - 1, 3)]
        rows = jnp.concatenate([three[k] for k in range(3)], axis=1)
        product = jnp.dot(rows, table, preferred_element_type=F32)
        low = product[:TRACERS, ROW:] + product[TRACERS:, :ROW] + product[TRACERS:, ROW:]
        return product[:TRACERS, :ROW] + low

    def average(source, level, pair):
        four = source[level, pl.ds(2 * pair + 1, 4)]
        rows = jnp.concatenate([four[k] for k in range(4)], axis=1)
        product = jnp.dot(rows, shared_pair(pair), preferred_element_type=F32)
        return (product[:TRACERS] + product[TRACERS:]) * inverse[pair]

    def up_copy():
        return pltpu.make_async_remote_copy(
            src_ref=result.at[0],
            dst_ref=above,
            send_sem=send_up,
            recv_sem=recv_up,
            device_id={"lev": group - 1},
            device_id_type=MESH,
        )

    def first_part(side):
        slot = slot_here[side]
        for copy in dep_copies(side, slot):
            copy.wait_recv()
        if side == far:

            @pl.when(first)
            def _():
                send(far)

        inner = 3 - 3 * (slot // 2)
        prepare(slot, 0, 1 - slot // 2, 3)
        prepare(slot, 1, inner, 1)
        pair = 3 * (slot // 2)
        for k in range(2):
            extended = 2 + 2 * pair + k
            build_shared(slot, extended % 4, extended - 2)
        for k in range(2):
            invert_masses(2 * (slot // 2) + k)

    def arrived(side, level):
        slot = slot_here[side]
        for k in range(3):
            moved1_unit(slot, 1 - slot // 2 + k, level)
        moved2_unit(slot, 3 - 3 * (slot // 2), level)
        field_copy(side, slot, level).wait_recv()
        for row in range(4):
            rows0[level, 4 * slot + row] = split(fields[slot, level, :, ROW * row : ROW * (row + 1)])

    def step(level, start1, count1, pairs, start2, count2):
        for k in range(count1):
            moved1[level, start1 + k] = split(interpolate(rows0, level, start1 + k, start1 + k - 1))
        for k in range(2):
            both = split(average(moved1, level, pairs + k))
            rows1[level, 2 + 2 * (pairs + k)] = both[:, :ROW]
            rows1[level, 3 + 2 * (pairs + k)] = both[:, ROW:]
        for k in range(count2):
            moved2[level, start2 + k] = split(interpolate(rows1, level, start2 + k, start2 + k + 7))

    def near_arrivals(half, carry):
        for k in range(2):
            arrived(near, 2 * half + k)
        for k in range(2):
            for row in range(6):
                level, extended = 2 * half + k, 5 - 4 * odd + row
                moved1[level, extended] = split(interpolate(rows0, level, extended, extended - 1))
        return carry

    def near_rest():
        for k in range(2):
            pair = 2 - 2 * odd + k
            levels = [moved1[level, pl.ds(2 * pair + 1, 4)] for level in range(LEVELS)]
            rows = jnp.concatenate([jnp.concatenate([four[j] for j in range(4)], axis=1) for four in levels], axis=0)
            product = jnp.dot(rows, shared_pair(pair), preferred_element_type=F32)
            for level in range(LEVELS):
                high = product[2 * TRACERS * level : 2 * TRACERS * level + TRACERS]
                low = product[2 * TRACERS * level + TRACERS : 2 * TRACERS * (level + 1)]
                both = split((high + low) * inverse[pair])
                rows1[level, 2 + 2 * pair] = both[:, :ROW]
                rows1[level, 3 + 2 * pair] = both[:, ROW:]
        for level in range(LEVELS):
            for k in range(2):
                extended = 7 - 4 * odd + k
                moved2[level, extended] = split(interpolate(rows1, level, extended, extended + 7))

    def far_level(level, carry):
        arrived(far, level)
        step(level, 1 + 6 * odd, 4, 2 * odd, 3 + 2 * odd, 4)
        for pair in (1, 2):
            at = 256 * (pair - 1)
            result[level, :, at : at + 256] = average(moved2, level, pair)

        @pl.when((level == 0) & (group > 0))
        def _():
            up_copy().start()

        return carry

    first_part(near)
    lax.fori_loop(0, LEVELS // 2, near_arrivals, 0)
    near_rest()
    first_part(far)
    lax.fori_loop(0, LEVELS, far_level, 0)

    for level in range(LEVELS - 1):
        field = result[level]
        out[level] = field + lifts[pl.ds(level, 1), :] * (result[level + 1] - field)

    for side in (far, near):
        for copy in dep_copies(side, slot_there[side]):
            copy.wait_send()
        for level in range(LEVELS):
            field_copy(side, slot_there[side], level).wait_send()

    end = LEVELS - 1

    @pl.when(group > 0)
    def _():
        up_copy().wait_send()

    @pl.when(group < groups - 1)
    def _():
        up_copy().wait_recv()
        field = result[end]
        out[end] = field + lifts[pl.ds(end, 1), :] * (above[...] - field)

    @pl.when(group == groups - 1)
    def _():
        field = result[end]
        out[end] = field + lifts[pl.ds(end, 1), :] * (field - field)


def local(tracers, owners, source_elements, ref_coords, node_mass, neighbours, lift_fraction):
    dma = pltpu.SemaphoreType.DMA
    return pl.pallas_call(
        kernel,
        out_shape=jax.ShapeDtypeStruct(tracers.shape, F32),
        in_specs=[pl.BlockSpec(memory_space=pltpu.HBM)] * 7,
        out_specs=pl.BlockSpec(memory_space=pltpu.VMEM),
        scratch_shapes=[
            pltpu.VMEM((3, LEVELS, TRACERS, BLOCK), F32),
            pltpu.VMEM((3, 2, LEVELS, BLOCK), jnp.int32),
            pltpu.VMEM((3, 2, LEVELS, BLOCK), jnp.int32),
            pltpu.VMEM((3, 2, 2, LEVELS, BLOCK), F32),
            pltpu.VMEM((3, 1, BLOCK), F32),
            pltpu.VMEM((3, 3, BLOCK), jnp.int32),
            pltpu.VMEM((LEVELS, BLOCK), F32),
            pltpu.VMEM((3, 2, LEVELS, 3, BLOCK), F32),
            pltpu.VMEM((LEVELS, 16, 3, 16, ROW), F32),
            pltpu.VMEM((8, 384, ROW), BF16),
            pltpu.VMEM((4, 1, 256), F32),
            pltpu.VMEM((LEVELS, 12, 2 * TRACERS, ROW), BF16),
            pltpu.VMEM((LEVELS, 12, 2 * TRACERS, ROW), BF16),
            pltpu.VMEM((LEVELS, 12, 2 * TRACERS, ROW), BF16),
            pltpu.VMEM((LEVELS, 12, 2 * TRACERS, ROW), BF16),
            pltpu.VMEM((LEVELS, TRACERS, BLOCK), F32),
            pltpu.VMEM((TRACERS, BLOCK), F32),
            dma((7,)),
            dma((2, 8)),
            dma((2, 8)),
            dma((2, LEVELS)),
            dma((2, LEVELS)),
            dma,
            dma,
        ],
        compiler_params=pltpu.CompilerParams(
            collective_id=0, has_side_effects=True, vmem_limit_bytes=32 << 20
        ),
    )(*(pltpu.with_memory_space_constraint(x, pltpu.HBM) for x in (tracers, owners, source_elements, ref_coords, node_mass.reshape(1, -1), neighbours, lift_fraction)))


def solution(mesh):
    in_specs = (
        P("lev", None, "sfc"),
        P(None, "lev", "sfc"),
        P(None, "lev", "sfc"),
        P(None, None, "lev", "sfc"),
        P("sfc"),
        P(None, "sfc"),
        P("lev", "sfc"),
    )
    out_specs = P("lev", None, "sfc")
    return jax.shard_map(local, mesh=mesh, in_specs=in_specs, out_specs=out_specs, check_vma=False)
```

```python
import functools

import jax
import jax.numpy as jnp
from jax import lax
from jax.experimental import pallas as pl
from jax.experimental.pallas import tpu as pltpu
from jax.sharding import PartitionSpec as P

GLL_POINTS = (-1.0, -0.4472135954999579, 0.4472135954999579, 1.0)
MESH = pl.DeviceIdType.MESH
BF16 = jnp.bfloat16
F32 = jnp.float32
LEVELS = 4
TRACERS = 40
ROW = 128
BLOCK = 512


def basis_tables():
    node = lax.broadcasted_iota(jnp.int32, (16, ROW), 0)

    def pick(index, values):
        out = jnp.full((16, ROW), values[3], F32)
        for k in range(3):
            out = jnp.where(index == k, values[k], out)
        return out

    others = [[x for k, x in enumerate(GLL_POINTS) if k != i] for i in range(4)]
    scale = []
    for i in range(4):
        product = 1.0
        for x in others[i]:
            product *= GLL_POINTS[i] - x
        scale.append(1.0 / product)
    first, second = node >> 2, node & 3
    points_a = [pick(first, [others[i][k] for i in range(4)]) for k in range(3)]
    points_b = [pick(second, [others[i][k] for i in range(4)]) for k in range(3)]
    return points_a, points_b, pick(first, scale) * pick(second, scale)


def split(values):
    high = values.astype(BF16).astype(F32)
    return jnp.concatenate([high, values - high], axis=0).astype(BF16)


def spread(row):
    return jnp.broadcast_to(row, (16, ROW))


def kernel(
    tracers, owners, elements, coords, mass, neighbours, lift,
    out,
    fields, own_ids, elem_ids, refs, masses, copies, lifts, prepared, packed, message,
    units, shared, inverse, moved1, rows1, moved2, result, above,
    local_sem, send_dep, recv_dep, send_field, recv_field, send_up, recv_up, token,
):
    me = lax.axis_index("sfc")
    peers = lax.axis_size("sfc")
    group = lax.axis_index("lev")
    groups = lax.axis_size("lev")
    after = lax.rem(me + 1, peers)
    before = lax.rem(me + peers - 1, peers)

    odd = lax.rem(me, 2)
    far, near = 0, 1
    device = (jnp.where(odd == 1, after, before), jnp.where(odd == 1, before, after))
    slot_here = (2 * odd, 2 - 2 * odd)
    slot_there = (2 - 2 * odd, 2 * odd)

    first, last = me == 0, me == peers - 1

    barrier = pltpu.get_barrier_semaphore()
    pl.semaphore_signal(barrier, inc=1, device_id={"sfc": device[near]}, device_id_type=MESH)

    @pl.when(jnp.logical_not(last))
    def _():
        pl.semaphore_signal(barrier, inc=1, device_id={"sfc": device[far]}, device_id_type=MESH)

    @pl.when(group < groups - 1)
    def _():
        pl.semaphore_signal(barrier, inc=1, device_id={"lev": group + 1}, device_id_type=MESH)

    local = []

    def fetch(source, target):
        copy = pltpu.make_async_copy(source, target, local_sem.at[len(local)])
        copy.start()
        local.append(copy)

    fetch(owners, own_ids)
    fetch(elements, elem_ids)
    fetch(coords, refs)
    fetch(mass, masses)
    fetch(neighbours, copies)

    pl.semaphore_wait(barrier, 1 + jnp.where(first, 0, 1) + jnp.where(group > 0, 1, 0))

    @pl.when(last)
    def _():
        pl.semaphore_signal(token, inc=1, device_id={"sfc": device[far]}, device_id_type=MESH)


    def message_copy(side, slot):
        return pltpu.make_async_remote_copy(
            src_ref=packed.at[side],
            dst_ref=message.at[slot],
            send_sem=send_dep.at[side],
            recv_sem=recv_dep.at[side],
            device_id={"sfc": device[side]},
            device_id_type=MESH,
        )

    def field_copy(side, slot, level):
        return pltpu.make_async_remote_copy(
            src_ref=tracers.at[level],
            dst_ref=fields.at[slot, level],
            send_sem=send_field.at[side, level],
            recv_sem=recv_field.at[side, level],
            device_id={"sfc": device[side]},
            device_id_type=MESH,
        )

    points_a, points_b, scale = basis_tables()
    row_mask = 4 * peers - 1
    point_mask = BLOCK * peers - 1
    node = lax.broadcasted_iota(jnp.int32, (16, ROW), 0)
    lane = lax.broadcasted_iota(jnp.int32, (16, ROW), 1)
    zero = jnp.zeros((16, ROW), BF16)
    own_elem = (8 + (lane >> 4)).astype(F32).astype(BF16)
    own_pick = jnp.where((lane & 15) == node, 1.0, 0.0).astype(BF16)

    def prepare(step):
        row = lax.broadcasted_iota(jnp.int32, (LEVELS, BLOCK), 1) // ROW
        elem = elem_ids[step]
        offset = own_ids[step] * 4 + (elem >> 3) - (me * 4 - 1 + row)
        code = ((offset & row_mask) * 8 + (elem & 7)).astype(F32)
        for level in range(LEVELS):
            prepared[step, level, 0:1] = code[level : level + 1]
            prepared[step, level, 1:2] = refs[step, 0, level : level + 1]
            prepared[step, level, 2:3] = refs[step, 1, level : level + 1]

    def pack(side):
        slot = slot_there[side]
        start = (2 - slot) * 64
        three = pl.ds(pl.multiple_of(start, ROW), 3 * ROW)
        one = pl.ds(pl.multiple_of(3 * start, ROW), ROW)
        two = pl.ds(pl.multiple_of(2 * start, ROW), 2 * ROW)
        for level in range(LEVELS):
            packed[side, level, 0:3, 0:384] = prepared[0, level, 0:3, three]
            packed[side, level, 0:3, 384:512] = prepared[1, level, 0:3, one]
        packed[side, 0, 3:4, 0:384] = masses[:, three]
        packed[side, 0, 3:4, 384:512] = jnp.zeros((1, ROW), F32)
        for number in range(3):
            packed[side, 1 + number, 3:4, 0:256] = copies[number : number + 1, two].astype(F32)
            packed[side, 1 + number, 3:4, 256:512] = jnp.zeros((1, 256), F32)

    for copy in local[:5]:
        copy.wait()
    for step in range(2):
        prepare(step)
    pack(far)

    @pl.when(jnp.logical_not(first))
    def _():
        message_copy(far, slot_there[far]).start()
        for level in range(LEVELS):
            field_copy(far, slot_there[far], level).start()

    fetch(lift, lifts)
    fetch(tracers, fields.at[1])
    pack(near)
    message_copy(near, slot_there[near]).start()
    for level in range(LEVELS):
        field_copy(near, slot_there[near], level).start()

    def build_unit(point, weight_row, level, unit):
        a = spread(point[1:2])
        b = spread(point[2:3])
        weight = spread(weight_row) * scale
        for x in points_a:
            weight = weight * (a - x)
        for x in points_b:
            weight = weight * (b - x)
        high = weight.astype(BF16).astype(F32)
        units[level, unit, 0] = spread(point[0:1])
        units[level, unit, 1] = high
        units[level, unit, 2] = weight - high

    def build_shared(slot, row, links, place):
        first_node = ((me + (slot - 1)) * 4 + (row - 1)) * ROW
        codes, picks = [], []
        for number in range(3):
            copy = links[number]
            offset = (copy - first_node) & point_mask
            code = jnp.where(copy >= 0, offset >> 4, -1)
            codes.append(spread(code.astype(F32)).astype(BF16))
            picks.append(jnp.where(spread(offset & 15) == node, 1.0, 0.0).astype(BF16))
        for number in range(24):
            count = jnp.asarray(number, BF16)
            value = None
            for code, pick in zip(codes, picks):
                term = jnp.where(code == count, pick, zero)
                value = term if value is None else value + term
            if 8 <= number < 16:
                value = value + jnp.where(own_elem == count, own_pick, zero)
            shared[place, pl.ds(16 * number, 16), :] = value

    def lanes_of(row):
        return slice(ROW * row, ROW * (row + 1))

    def own_level(level, carry):
        for row in range(4):
            at = lanes_of(row)
            build_unit(prepared[0, level, 0:3, at], masses[:, at], level, 3 + row)
            build_unit(prepared[1, level, 0:3, at], masses[:, at], level, 11 + row)
        return carry

    lax.fori_loop(0, LEVELS, own_level, 0)
    for row in range(4):
        build_shared(1, row, [copies[k : k + 1, lanes_of(row)] for k in range(3)], 2 + row)
    for copy in local[5:]:
        copy.wait()

    blank = jnp.zeros((ROW, ROW), BF16)

    def shared_pair(pair):
        first = jnp.concatenate([shared[2 * pair], blank], axis=0)
        second = jnp.concatenate([blank, shared[2 * pair + 1]], axis=0)
        return jnp.concatenate([first, second], axis=1)

    piece = lax.broadcasted_iota(jnp.int32, (16, ROW), 0)

    def mass_parts(row):
        whole = spread(row)
        high = whole.astype(BF16).astype(F32)
        middle = (whole - high).astype(BF16).astype(F32)
        low = whole - high - middle
        mixed = jnp.where(piece == 0, high, jnp.where(piece == 1, middle, jnp.where(piece == 2, low, 0.0)))
        return mixed.astype(BF16)

    def invert_masses(rows, pair):
        parts = jnp.concatenate([mass_parts(row) for row in rows], axis=1)
        total = jnp.dot(parts, shared_pair(pair), preferred_element_type=F32)
        inverse[pair] = 1.0 / jnp.sum(total, axis=0, keepdims=True)

    def interpolate(rows, level, unit):
        code, high, low = (units[level, unit, part].astype(BF16) for part in range(3))
        hits = [code == jnp.asarray(number, BF16) for number in range(24)]
        table = jnp.concatenate(
            [
                jnp.concatenate([jnp.where(hit, part, zero) for hit in hits], axis=0)
                for part in (high, low)
            ],
            axis=1,
        )
        product = jnp.dot(jnp.concatenate(rows, axis=1), table, preferred_element_type=F32)
        low = product[:TRACERS, ROW:] + product[TRACERS:, :ROW] + product[TRACERS:, ROW:]
        return product[:TRACERS, :ROW] + low

    def average(rows, pair):
        product = jnp.dot(jnp.concatenate(rows, axis=1), shared_pair(pair), preferred_element_type=F32)
        return (product[:TRACERS] + product[TRACERS:]) * inverse[pair]

    def up_copy():
        return pltpu.make_async_remote_copy(
            src_ref=result.at[0],
            dst_ref=above,
            send_sem=send_up,
            recv_sem=recv_up,
            device_id={"lev": group - 1},
            device_id_type=MESH,
        )

    def first_part(side, slot):
        message_copy(side, slot).wait_recv()
        below = slot == 2
        for k in range(2):
            links = [message[slot, 1 + number, 3:4, lanes_of(k)].astype(jnp.int32) for number in range(3)]
            build_shared(slot, k if below else 2 + k, links, (6 if below else 0) + k)
        theirs = [message[slot, 0, 3:4, lanes_of(k)] for k in range(3)]
        own = [masses[:, lanes_of(row)] for row in range(4)]
        rows = own + theirs if below else theirs + own
        for k in range(2):
            begin = (1 if below else 0) + 2 * k
            invert_masses(rows[begin : begin + 4], (2 if below else 0) + k)

    def arrived(side, slot, level):
        weight_rows = [message[slot, 0, 3:4, lanes_of(k)] for k in range(3)]
        for k in range(3):
            build_unit(message[slot, level, 0:3, lanes_of(k)], weight_rows[k], level, (7 if slot == 2 else 0) + k)
        beside = 0 if slot == 2 else 2
        build_unit(message[slot, level, 0:3, lanes_of(3)], weight_rows[beside], level, 15 if slot == 2 else 10)
        field_copy(side, slot, level).wait_recv()

    def field_row(extended, level):
        row = extended % 4
        return split(fields[extended // 4, level, :, ROW * row : ROW * (row + 1)])

    def around(rows, extended, count):
        return [rows[extended + k - 1] for k in range(count)]

    def near_part(parity):
        slot, begin, first_pair = 2 - 2 * parity, 5 - 4 * parity, 2 - 2 * parity
        first_part(near, slot)

        def arrivals(half, carry):
            levels = [2 * half + k for k in range(2)]
            for level in levels:
                arrived(near, slot, level)
            for level in levels:
                rows = {e: field_row(e, level) for e in range(begin - 1, begin + 7)}
                for e in range(begin, begin + 6):
                    moved1[level, e] = split(interpolate(around(rows, e, 3), level, e - 1))
            return carry

        lax.fori_loop(0, LEVELS // 2, arrivals, 0)
        fields1 = [{} for _ in range(LEVELS)]
        for pair in (first_pair, first_pair + 1):
            e = 2 + 2 * pair
            rows = [jnp.concatenate([moved1[level, e + k - 1] for k in range(4)], axis=1) for level in range(LEVELS)]
            product = jnp.dot(jnp.concatenate(rows, axis=0), shared_pair(pair), preferred_element_type=F32)
            for level in range(LEVELS):
                start = 2 * TRACERS * level
                total = product[start : start + TRACERS] + product[start + TRACERS : start + 2 * TRACERS]
                both = split(total * inverse[pair])
                for k in range(2):
                    fields1[level][e + k] = both[:, ROW * k : ROW * (k + 1)]
                    rows1[level, e + k] = fields1[level][e + k]
        for level in range(LEVELS):
            for e in (begin + 2, begin + 3):
                moved2[level, e] = split(interpolate(around(fields1[level], e, 3), level, e + 7))

    def remap(level):
        field = result[level]
        out[level] = field + lifts[pl.ds(level, 1), :] * (result[level + 1] - field)

    def far_part(parity):
        slot, begin, first_pair, begin2 = 2 * parity, 1 + 6 * parity, 2 * parity, 3 + 2 * parity
        first_part(far, slot)

        def one_level(level, carry):
            arrived(far, slot, level)
            rows = {e: field_row(e, level) for e in range(begin - 1, begin + 5)}
            moved = {e: split(interpolate(around(rows, e, 3), level, e - 1)) for e in range(begin, begin + 4)}
            for e in (5, 6):
                moved[e] = moved1[level, e]
            rows = {e: rows1[level, e] for e in (6 - 2 * parity, 7 - 2 * parity)}
            for pair in (first_pair, first_pair + 1):
                e = 2 + 2 * pair
                both = split(average(around(moved, e, 4), pair))
                rows[e], rows[e + 1] = both[:, :ROW], both[:, ROW:]
            moved = {e: moved2[level, e] for e in (7 - 4 * parity, 8 - 4 * parity)}
            for e in range(begin2, begin2 + 4):
                moved[e] = split(interpolate(around(rows, e, 3), level, e + 7))
            for pair in (1, 2):
                at = 256 * (pair - 1)
                result[level, :, at : at + 256] = average(around(moved, 2 + 2 * pair, 4), pair)

            @pl.when((level == 0) & (group > 0))
            def _():
                up_copy().start()

            return carry

        lax.fori_loop(0, LEVELS, one_level, 0)

    def by_parity(part):
        @pl.when(odd == 0)
        def _():
            part(0)

        @pl.when(odd == 1)
        def _():
            part(1)

    by_parity(near_part)

    @pl.when(first)
    def _():
        pl.semaphore_wait(token, 1)
        message_copy(far, slot_there[far]).start()
        for level in range(LEVELS):
            field_copy(far, slot_there[far], level).start()

    by_parity(far_part)

    for level in range(LEVELS - 1):
        remap(level)

    for side in (far, near):
        message_copy(side, slot_there[side]).wait_send()
        for level in range(LEVELS):
            field_copy(side, slot_there[side], level).wait_send()

    end = LEVELS - 1

    @pl.when(group > 0)
    def _():
        up_copy().wait_send()

    @pl.when(group < groups - 1)
    def _():
        up_copy().wait_recv()
        field = result[end]
        out[end] = field + lifts[pl.ds(end, 1), :] * (above[...] - field)

    @pl.when(group == groups - 1)
    def _():
        field = result[end]
        out[end] = field + lifts[pl.ds(end, 1), :] * (field - field)


def local(tracers, owners, source_elements, ref_coords, node_mass, neighbours, lift_fraction):
    dma = pltpu.SemaphoreType.DMA
    return pl.pallas_call(
        kernel,
        out_shape=jax.ShapeDtypeStruct(tracers.shape, F32),
        in_specs=[pl.BlockSpec(memory_space=pltpu.HBM)] * 7,
        out_specs=pl.BlockSpec(memory_space=pltpu.VMEM),
        scratch_shapes=[
            pltpu.VMEM((3, LEVELS, TRACERS, BLOCK), F32),
            pltpu.VMEM((2, LEVELS, BLOCK), jnp.int32),
            pltpu.VMEM((2, LEVELS, BLOCK), jnp.int32),
            pltpu.VMEM((2, 2, LEVELS, BLOCK), F32),
            pltpu.VMEM((1, BLOCK), F32),
            pltpu.VMEM((3, BLOCK), jnp.int32),
            pltpu.VMEM((LEVELS, BLOCK), F32),
            pltpu.VMEM((2, LEVELS, 3, BLOCK), F32),
            pltpu.VMEM((2, LEVELS, 4, BLOCK), F32),
            pltpu.VMEM((3, LEVELS, 4, BLOCK), F32),
            pltpu.VMEM((LEVELS, 16, 3, 16, ROW), F32),
            pltpu.VMEM((8, 384, ROW), BF16),
            pltpu.VMEM((4, 1, 256), F32),
            pltpu.VMEM((LEVELS, 12, 2 * TRACERS, ROW), BF16),
            pltpu.VMEM((LEVELS, 12, 2 * TRACERS, ROW), BF16),
            pltpu.VMEM((LEVELS, 12, 2 * TRACERS, ROW), BF16),
            pltpu.VMEM((LEVELS, TRACERS, BLOCK), F32),
            pltpu.VMEM((TRACERS, BLOCK), F32),
            dma((7,)),
            dma((2,)),
            dma((2,)),
            dma((2, LEVELS)),
            dma((2, LEVELS)),
            dma,
            dma,
            pltpu.SemaphoreType.REGULAR,
        ],
        compiler_params=pltpu.CompilerParams(
            collective_id=0, has_side_effects=True, vmem_limit_bytes=32 << 20
        ),
    )(*(pltpu.with_memory_space_constraint(x, pltpu.HBM) for x in (tracers, owners, source_elements, ref_coords, node_mass.reshape(1, -1), neighbours, lift_fraction)))


def solution(mesh):
    in_specs = (
        P("lev", None, "sfc"),
        P(None, "lev", "sfc"),
        P(None, "lev", "sfc"),
        P(None, None, "lev", "sfc"),
        P("sfc"),
        P(None, "sfc"),
        P("lev", "sfc"),
    )
    out_specs = P("lev", None, "sfc")
    return jax.shard_map(local, mesh=mesh, in_specs=in_specs, out_specs=out_specs, check_vma=False)
```

```python
import functools

import jax
import jax.numpy as jnp
from jax import lax
from jax.experimental import pallas as pl
from jax.experimental.pallas import tpu as pltpu
from jax.sharding import PartitionSpec as P

GLL_POINTS = (-1.0, -0.4472135954999579, 0.4472135954999579, 1.0)
MESH = pl.DeviceIdType.MESH
BF16 = jnp.bfloat16
F32 = jnp.float32
LEVELS = 4
TRACERS = 40
ROW = 128
BLOCK = 512


def basis_tables():
    node = lax.broadcasted_iota(jnp.int32, (16, ROW), 0)

    def pick(index, values):
        out = jnp.full((16, ROW), values[3], F32)
        for k in range(3):
            out = jnp.where(index == k, values[k], out)
        return out

    others = [[x for k, x in enumerate(GLL_POINTS) if k != i] for i in range(4)]
    scale = []
    for i in range(4):
        product = 1.0
        for x in others[i]:
            product *= GLL_POINTS[i] - x
        scale.append(1.0 / product)
    first, second = node >> 2, node & 3
    points_a = [pick(first, [others[i][k] for i in range(4)]) for k in range(3)]
    points_b = [pick(second, [others[i][k] for i in range(4)]) for k in range(3)]
    return points_a, points_b, pick(first, scale) * pick(second, scale)


def split(values):
    high = values.astype(BF16).astype(F32)
    return jnp.concatenate([high, values - high], axis=0).astype(BF16)


def spread(row):
    return jnp.broadcast_to(row, (16, ROW))


def kernel(
    tracers, owners, elements, coords, mass, neighbours, lift,
    out,
    fields, own_ids, elem_ids, refs, masses, copies, lifts, prepared, packed, message,
    units, shared, inverse, moved1, rows1, moved2, result, above,
    local_sem, send_dep, recv_dep, send_field, recv_field, send_half, recv_half, send_up, recv_up, token,
):
    me = lax.axis_index("sfc")
    peers = lax.axis_size("sfc")
    group = lax.axis_index("lev")
    groups = lax.axis_size("lev")
    after = lax.rem(me + 1, peers)
    before = lax.rem(me + peers - 1, peers)

    odd = lax.rem(me, 2)
    far, near = 0, 1
    device = (jnp.where(odd == 1, after, before), jnp.where(odd == 1, before, after))
    slot_here = (2 * odd, 2 - 2 * odd)
    slot_there = (2 - 2 * odd, 2 * odd)

    first, last = me == 0, me == peers - 1

    barrier = pltpu.get_barrier_semaphore()
    pl.semaphore_signal(barrier, inc=1, device_id={"sfc": device[near]}, device_id_type=MESH)

    @pl.when(jnp.logical_not(last))
    def _():
        pl.semaphore_signal(barrier, inc=1, device_id={"sfc": device[far]}, device_id_type=MESH)

    @pl.when(group < groups - 1)
    def _():
        pl.semaphore_signal(barrier, inc=1, device_id={"lev": group + 1}, device_id_type=MESH)

    local = []

    def fetch(source, target):
        copy = pltpu.make_async_copy(source, target, local_sem.at[len(local)])
        copy.start()
        local.append(copy)

    fetch(owners, own_ids)
    fetch(elements, elem_ids)
    fetch(coords, refs)
    fetch(mass, masses)
    fetch(neighbours, copies)

    pl.semaphore_wait(barrier, 1 + jnp.where(first, 0, 1) + jnp.where(group > 0, 1, 0))

    @pl.when(last)
    def _():
        pl.semaphore_signal(token, inc=1, device_id={"sfc": device[far]}, device_id_type=MESH)


    def message_copy(side, slot):
        return pltpu.make_async_remote_copy(
            src_ref=packed.at[side],
            dst_ref=message.at[slot],
            send_sem=send_dep.at[side],
            recv_sem=recv_dep.at[side],
            device_id={"sfc": device[side]},
            device_id_type=MESH,
        )

    def field_copy(side, slot, level):
        return pltpu.make_async_remote_copy(
            src_ref=tracers.at[level],
            dst_ref=fields.at[slot, level],
            send_sem=send_field.at[side, level],
            recv_sem=recv_field.at[side, level],
            device_id={"sfc": device[side]},
            device_id_type=MESH,
        )

    def half_copy(slot, part):
        start = (2 - slot) * ROW if part == 0 else slot * ROW
        lanes = pl.ds(start if isinstance(start, int) else pl.multiple_of(start, ROW), 2 * ROW)
        return pltpu.make_async_remote_copy(
            src_ref=tracers.at[0, :, lanes],
            dst_ref=fields.at[slot, 0, :, lanes],
            send_sem=send_half.at[part],
            recv_sem=recv_half.at[part],
            device_id={"sfc": device[far]},
            device_id_type=MESH,
        )

    def far_copies():
        slot = slot_there[far]
        halves = [half_copy(slot, part) for part in range(2)]
        return [message_copy(far, slot)] + halves + [field_copy(far, slot, level) for level in range(1, LEVELS)]

    points_a, points_b, scale = basis_tables()
    row_mask = 4 * peers - 1
    point_mask = BLOCK * peers - 1
    node = lax.broadcasted_iota(jnp.int32, (16, ROW), 0)
    lane = lax.broadcasted_iota(jnp.int32, (16, ROW), 1)
    zero = jnp.zeros((16, ROW), BF16)
    own_elem = (8 + (lane >> 4)).astype(F32).astype(BF16)
    own_pick = jnp.where((lane & 15) == node, 1.0, 0.0).astype(BF16)

    def prepare(step):
        row = lax.broadcasted_iota(jnp.int32, (LEVELS, BLOCK), 1) // ROW
        elem = elem_ids[step]
        offset = own_ids[step] * 4 + (elem >> 3) - (me * 4 - 1 + row)
        code = ((offset & row_mask) * 8 + (elem & 7)).astype(F32)
        for level in range(LEVELS):
            prepared[step, level, 0:1] = code[level : level + 1]
            prepared[step, level, 1:2] = refs[step, 0, level : level + 1]
            prepared[step, level, 2:3] = refs[step, 1, level : level + 1]

    def pack(side):
        slot = slot_there[side]
        start = (2 - slot) * 64
        three = pl.ds(pl.multiple_of(start, ROW), 3 * ROW)
        one = pl.ds(pl.multiple_of(3 * start, ROW), ROW)
        two = pl.ds(pl.multiple_of(2 * start, ROW), 2 * ROW)
        for level in range(LEVELS):
            packed[side, level, 0:3, 0:384] = prepared[0, level, 0:3, three]
            packed[side, level, 0:3, 384:512] = prepared[1, level, 0:3, one]
        packed[side, 0, 3:4, 0:384] = masses[:, three]
        packed[side, 0, 3:4, 384:512] = jnp.zeros((1, ROW), F32)
        for number in range(3):
            packed[side, 1 + number, 3:4, 0:256] = copies[number : number + 1, two].astype(F32)
            packed[side, 1 + number, 3:4, 256:512] = jnp.zeros((1, 256), F32)

    for copy in local[:5]:
        copy.wait()
    for step in range(2):
        prepare(step)
    pack(far)

    @pl.when(jnp.logical_not(first))
    def _():
        for copy in far_copies():
            copy.start()

    fetch(lift, lifts)
    fetch(tracers, fields.at[1])
    pack(near)
    message_copy(near, slot_there[near]).start()
    for level in range(LEVELS):
        field_copy(near, slot_there[near], level).start()

    def build_unit(point, weight_row, level, unit):
        a = spread(point[1:2])
        b = spread(point[2:3])
        weight = spread(weight_row) * scale
        for x in points_a:
            weight = weight * (a - x)
        for x in points_b:
            weight = weight * (b - x)
        high = weight.astype(BF16).astype(F32)
        units[level, unit, 0] = spread(point[0:1])
        units[level, unit, 1] = high
        units[level, unit, 2] = weight - high

    def build_shared(slot, row, links, place):
        first_node = ((me + (slot - 1)) * 4 + (row - 1)) * ROW
        codes, picks = [], []
        for number in range(3):
            copy = links[number]
            offset = (copy - first_node) & point_mask
            code = jnp.where(copy >= 0, offset >> 4, -1)
            codes.append(spread(code.astype(F32)).astype(BF16))
            picks.append(jnp.where(spread(offset & 15) == node, 1.0, 0.0).astype(BF16))
        for number in range(24):
            count = jnp.asarray(number, BF16)
            value = None
            for code, pick in zip(codes, picks):
                term = jnp.where(code == count, pick, zero)
                value = term if value is None else value + term
            if 8 <= number < 16:
                value = value + jnp.where(own_elem == count, own_pick, zero)
            shared[place, pl.ds(16 * number, 16), :] = value

    def lanes_of(row):
        return slice(ROW * row, ROW * (row + 1))

    def own_level(level, carry):
        for row in range(4):
            at = lanes_of(row)
            build_unit(prepared[0, level, 0:3, at], masses[:, at], level, 3 + row)
            build_unit(prepared[1, level, 0:3, at], masses[:, at], level, 11 + row)
        return carry

    lax.fori_loop(0, LEVELS, own_level, 0)
    for row in range(4):
        build_shared(1, row, [copies[k : k + 1, lanes_of(row)] for k in range(3)], 2 + row)
    for copy in local[5:]:
        copy.wait()

    blank = jnp.zeros((ROW, ROW), BF16)

    def shared_pair(pair):
        first = jnp.concatenate([shared[2 * pair], blank], axis=0)
        second = jnp.concatenate([blank, shared[2 * pair + 1]], axis=0)
        return jnp.concatenate([first, second], axis=1)

    piece = lax.broadcasted_iota(jnp.int32, (16, ROW), 0)

    def mass_parts(row):
        whole = spread(row)
        high = whole.astype(BF16).astype(F32)
        middle = (whole - high).astype(BF16).astype(F32)
        low = whole - high - middle
        mixed = jnp.where(piece == 0, high, jnp.where(piece == 1, middle, jnp.where(piece == 2, low, 0.0)))
        return mixed.astype(BF16)

    def invert_masses(rows, pair):
        parts = jnp.concatenate([mass_parts(row) for row in rows], axis=1)
        total = jnp.dot(parts, shared_pair(pair), preferred_element_type=F32)
        inverse[pair] = 1.0 / jnp.sum(total, axis=0, keepdims=True)

    def interpolate(rows, level, unit):
        code, high, low = (units[level, unit, part].astype(BF16) for part in range(3))
        hits = [code == jnp.asarray(number, BF16) for number in range(24)]
        table = jnp.concatenate(
            [
                jnp.concatenate([jnp.where(hit, part, zero) for hit in hits], axis=0)
                for part in (high, low)
            ],
            axis=1,
        )
        product = jnp.dot(jnp.concatenate(rows, axis=1), table, preferred_element_type=F32)
        low = product[:TRACERS, ROW:] + product[TRACERS:, :ROW] + product[TRACERS:, ROW:]
        return product[:TRACERS, :ROW] + low

    def average(rows, pair):
        product = jnp.dot(jnp.concatenate(rows, axis=1), shared_pair(pair), preferred_element_type=F32)
        return (product[:TRACERS] + product[TRACERS:]) * inverse[pair]

    def up_copy(half):
        return pltpu.make_async_remote_copy(
            src_ref=result.at[0, :, pl.ds(256 * half, 256)],
            dst_ref=above.at[:, pl.ds(256 * half, 256)],
            send_sem=send_up.at[half],
            recv_sem=recv_up.at[half],
            device_id={"lev": group - 1},
            device_id_type=MESH,
        )

    def first_part(side, slot):
        message_copy(side, slot).wait_recv()
        below = slot == 2
        for k in range(2):
            links = [message[slot, 1 + number, 3:4, lanes_of(k)].astype(jnp.int32) for number in range(3)]
            build_shared(slot, k if below else 2 + k, links, (6 if below else 0) + k)
        theirs = [message[slot, 0, 3:4, lanes_of(k)] for k in range(3)]
        own = [masses[:, lanes_of(row)] for row in range(4)]
        rows = own + theirs if below else theirs + own
        for k in range(2):
            begin = (1 if below else 0) + 2 * k
            invert_masses(rows[begin : begin + 4], (2 if below else 0) + k)

    def their_units(slot, level):
        weight_rows = [message[slot, 0, 3:4, lanes_of(k)] for k in range(3)]
        for k in range(3):
            build_unit(message[slot, level, 0:3, lanes_of(k)], weight_rows[k], level, (7 if slot == 2 else 0) + k)
        beside = 0 if slot == 2 else 2
        build_unit(message[slot, level, 0:3, lanes_of(3)], weight_rows[beside], level, 15 if slot == 2 else 10)

    def arrived(side, slot, level):
        their_units(slot, level)
        field_copy(side, slot, level).wait_recv()

    def field_row(extended, level):
        row = extended % 4
        return split(fields[extended // 4, level, :, ROW * row : ROW * (row + 1)])

    def around(rows, extended, count):
        return [rows[extended + k - 1] for k in range(count)]

    def near_part(parity):
        slot, begin, first_pair = 2 - 2 * parity, 5 - 4 * parity, 2 - 2 * parity
        first_part(near, slot)

        def arrivals(half, carry):
            levels = [2 * half + k for k in range(2)]
            for level in levels:
                arrived(near, slot, level)
            for level in levels:
                rows = {e: field_row(e, level) for e in range(begin - 1, begin + 7)}
                for e in range(begin, begin + 6):
                    moved1[level, e] = split(interpolate(around(rows, e, 3), level, e - 1))
            return carry

        lax.fori_loop(0, LEVELS // 2, arrivals, 0)
        fields1 = [{} for _ in range(LEVELS)]
        for pair in (first_pair, first_pair + 1):
            e = 2 + 2 * pair
            rows = [jnp.concatenate([moved1[level, e + k - 1] for k in range(4)], axis=1) for level in range(LEVELS)]
            product = jnp.dot(jnp.concatenate(rows, axis=0), shared_pair(pair), preferred_element_type=F32)
            for level in range(LEVELS):
                start = 2 * TRACERS * level
                total = product[start : start + TRACERS] + product[start + TRACERS : start + 2 * TRACERS]
                both = split(total * inverse[pair])
                for k in range(2):
                    fields1[level][e + k] = both[:, ROW * k : ROW * (k + 1)]
                    rows1[level, e + k] = fields1[level][e + k]
        for level in range(LEVELS):
            for e in (begin + 2, begin + 3):
                moved2[level, e] = split(interpolate(around(fields1[level], e, 3), level, e + 7))

    def remap(level):
        field = result[level]
        out[level] = field + lifts[pl.ds(level, 1), :] * (result[level + 1] - field)

    def far_part(parity):
        slot, begin, first_pair, begin2 = 2 * parity, 1 + 6 * parity, 2 * parity, 3 + 2 * parity
        first_part(far, slot)

        def one_level(level, carry):
            arrived(far, slot, level)
            rows = {e: field_row(e, level) for e in range(begin - 1, begin + 5)}
            moved = {e: split(interpolate(around(rows, e, 3), level, e - 1)) for e in range(begin, begin + 4)}
            for e in (5, 6):
                moved[e] = moved1[level, e]
            rows = {e: rows1[level, e] for e in (6 - 2 * parity, 7 - 2 * parity)}
            for pair in (first_pair, first_pair + 1):
                e = 2 + 2 * pair
                both = split(average(around(moved, e, 4), pair))
                rows[e], rows[e + 1] = both[:, :ROW], both[:, ROW:]
            moved = {e: moved2[level, e] for e in (7 - 4 * parity, 8 - 4 * parity)}
            for e in range(begin2, begin2 + 4):
                moved[e] = split(interpolate(around(rows, e, 3), level, e + 7))
            for pair in (1, 2):
                at = 256 * (pair - 1)
                result[level, :, at : at + 256] = average(around(moved, 2 + 2 * pair, 4), pair)

            return carry

        their_units(slot, 0)
        moved = {e: moved1[0, e] for e in (5, 6)}
        fields1 = {e: rows1[0, e] for e in (6 - 2 * parity, 7 - 2 * parity)}
        last_moved = {e: moved2[0, e] for e in (7 - 4 * parity, 8 - 4 * parity)}
        rows = {e: field_row(e, 0) for e in (4 + 2 * parity, 5 + 2 * parity)}
        for part in range(2):
            half_copy(slot, part).wait_recv()
            near_row = 8 + 2 * part if parity else 2 - 2 * part
            for e in (near_row, near_row + 1):
                rows[e] = field_row(e, 0)
            e = 7 + 2 * part if parity else 3 - 2 * part
            for e in (e, e + 1):
                moved[e] = split(interpolate(around(rows, e, 3), 0, e - 1))
            pair = 2 + part if parity else 1 - part
            both = split(average(around(moved, 2 + 2 * pair, 4), pair))
            fields1[2 + 2 * pair], fields1[3 + 2 * pair] = both[:, :ROW], both[:, ROW:]
            e = 5 + 2 * part if parity else 5 - 2 * part
            for e in (e, e + 1):
                last_moved[e] = split(interpolate(around(fields1, e, 3), 0, e + 7))
            pair = 1 + part if parity else 2 - part
            at = 256 * (pair - 1)
            result[0, :, at : at + 256] = average(around(last_moved, 2 + 2 * pair, 4), pair)

            @pl.when(group > 0)
            def _(half=pair - 1):
                up_copy(half).start()

        lax.fori_loop(1, LEVELS, one_level, 0)

    def by_parity(part):
        @pl.when(odd == 0)
        def _():
            part(0)

        @pl.when(odd == 1)
        def _():
            part(1)

    by_parity(near_part)

    @pl.when(first)
    def _():
        pl.semaphore_wait(token, 1)
        for copy in far_copies():
            copy.start()

    by_parity(far_part)

    for level in range(LEVELS - 1):
        remap(level)

    for copy in far_copies():
        copy.wait_send()
    message_copy(near, slot_there[near]).wait_send()
    for level in range(LEVELS):
        field_copy(near, slot_there[near], level).wait_send()

    end = LEVELS - 1

    @pl.when(group > 0)
    def _():
        for half in range(2):
            up_copy(half).wait_send()

    @pl.when(group < groups - 1)
    def _():
        for half in range(2):
            up_copy(half).wait_recv()
        field = result[end]
        out[end] = field + lifts[pl.ds(end, 1), :] * (above[...] - field)

    @pl.when(group == groups - 1)
    def _():
        field = result[end]
        out[end] = field + lifts[pl.ds(end, 1), :] * (field - field)


def local(tracers, owners, source_elements, ref_coords, node_mass, neighbours, lift_fraction):
    dma = pltpu.SemaphoreType.DMA
    return pl.pallas_call(
        kernel,
        out_shape=jax.ShapeDtypeStruct(tracers.shape, F32),
        in_specs=[pl.BlockSpec(memory_space=pltpu.HBM)] * 7,
        out_specs=pl.BlockSpec(memory_space=pltpu.VMEM),
        scratch_shapes=[
            pltpu.VMEM((3, LEVELS, TRACERS, BLOCK), F32),
            pltpu.VMEM((2, LEVELS, BLOCK), jnp.int32),
            pltpu.VMEM((2, LEVELS, BLOCK), jnp.int32),
            pltpu.VMEM((2, 2, LEVELS, BLOCK), F32),
            pltpu.VMEM((1, BLOCK), F32),
            pltpu.VMEM((3, BLOCK), jnp.int32),
            pltpu.VMEM((LEVELS, BLOCK), F32),
            pltpu.VMEM((2, LEVELS, 3, BLOCK), F32),
            pltpu.VMEM((2, LEVELS, 4, BLOCK), F32),
            pltpu.VMEM((3, LEVELS, 4, BLOCK), F32),
            pltpu.VMEM((LEVELS, 16, 3, 16, ROW), F32),
            pltpu.VMEM((8, 384, ROW), BF16),
            pltpu.VMEM((4, 1, 256), F32),
            pltpu.VMEM((LEVELS, 12, 2 * TRACERS, ROW), BF16),
            pltpu.VMEM((LEVELS, 12, 2 * TRACERS, ROW), BF16),
            pltpu.VMEM((LEVELS, 12, 2 * TRACERS, ROW), BF16),
            pltpu.VMEM((LEVELS, TRACERS, BLOCK), F32),
            pltpu.VMEM((TRACERS, BLOCK), F32),
            dma((7,)),
            dma((2,)),
            dma((2,)),
            dma((2, LEVELS)),
            dma((2, LEVELS)),
            dma((2,)),
            dma((2,)),
            dma((2,)),
            dma((2,)),
            pltpu.SemaphoreType.REGULAR,
        ],
        compiler_params=pltpu.CompilerParams(
            collective_id=0, has_side_effects=True, vmem_limit_bytes=32 << 20
        ),
    )(*(pltpu.with_memory_space_constraint(x, pltpu.HBM) for x in (tracers, owners, source_elements, ref_coords, node_mass.reshape(1, -1), neighbours, lift_fraction)))


def solution(mesh):
    in_specs = (
        P("lev", None, "sfc"),
        P(None, "lev", "sfc"),
        P(None, "lev", "sfc"),
        P(None, None, "lev", "sfc"),
        P("sfc"),
        P(None, "sfc"),
        P("lev", "sfc"),
    )
    out_specs = P("lev", None, "sfc")
    return jax.shard_map(local, mesh=mesh, in_specs=in_specs, out_specs=out_specs, check_vma=False)
```
